256 devices in a mesh: dp: 4 (over x), sect: 2 (over core), ctx: 32 (over z, y).
Axes of the slice: x: 4, y: 4, z: 8, core: 2. Of those that a mesh axis runs over, the one named last changes fastest.
Arguments:
- features: float32 [8, 2048, 2048], P('dp', 'ctx'), may hold values from -6 to 6
- rewards: float32 [8, 2048], P('dp', 'ctx'), may hold values from -0.8 to 0.8
- done_flags: int32 [8, 2048], P('dp', 'ctx'), may hold values 0 or 1
- traj_len: int32 [8], replicated, may hold values from 512 to 2048, as said below
- decay_rate: float32 [2, 8, 2048], P('sect'), may hold values from 9.765625e-06 to 0.03
- input_gain: float32 [2, 8, 2048], P('sect'), may hold values from -4 to 4
- output_gain: float32 [2, 8, 2048], P('sect'), may hold values from -2 to 2
- value_head: float32 [2048], replicated, may hold values from -0.125 to 0.125
Outputs:
- section_input_grad: float32 [2, 8, 2048, 2048], P('sect', 'dp', 'ctx')
- grad_input_gain: float32 [2, 8, 2048], P('sect', None, 'ctx')
- grad_output_gain: float32 [2, 8, 2048], P('sect', None, 'ctx')
The draws below stay inside these ranges and needn't reach their ends.
Inputs may be any that keep to these rules, and one draw needn't show every extreme that they name: `traj_len`: some trajectory uses all 2048 slots.
All inputs are finite; a program needn't handle non-finite values. No bound on the sum of `done_flags` on one device may be relied on, other than what follows from the above.
Results may differ from the reference program's by a relative error of at most 0.0003.
Values sent between devices are 32-bit elements; how exact they have to be, the bound alone decides.
No kernel may reach another device: no remote copies, remote signals or barrier semaphores. Data moves between devices by JAX's collectives and lax.ppermute only.
A program may use at most 128 MiB of HBM per device.

```python
import math
import jax
import jax.numpy as jnp
from jax import lax

D = 2048
K = 8
SECTIONS = 2
TRAJ = 8
LENGTH = 2048


def draw_traj_len(key, part):
    key = jax.random.fold_in(key, 11)
    spread = jax.random.randint(key, (TRAJ,), LENGTH // 4, LENGTH + 1)
    chosen = jax.random.randint(jax.random.fold_in(key, 5), (), 0, TRAJ)
    return jnp.where(jnp.arange(TRAJ) == chosen, LENGTH, spread).astype(jnp.int32)


def plant(entries, own_key, least, high):
    spot = [jax.random.randint(jax.random.fold_in(own_key, axis), (), 0, length) for axis, length in enumerate(entries.shape)]
    longest = entries.shape.index(max(entries.shape))
    next_to = spot[:longest] + [(spot[longest] + 1) % entries.shape[longest]] + spot[longest + 1:]
    return entries.at[tuple(spot)].set(least).at[tuple(next_to)].set(high)


def level_of(rng, shape, split, least, largest):
    loudness, own = 1.0, jax.random.fold_in(rng, 6)
    for dim, parts in split:
        draws = jnp.exp(jax.random.uniform(jax.random.fold_in(own, dim), (parts,), jnp.float32, least / len(split), largest / len(split)))
        loudness = loudness * jnp.repeat(draws, shape[dim] // parts).reshape([-1 if axis == dim else 1 for axis in range(len(shape))])
    return loudness


def scatter_about(stream_key, extent, deviation, bound, pieces=(), held_as=jnp.bfloat16):
    drawn = jax.random.normal(stream_key, extent, jnp.float32) * deviation
    if len(pieces) > 0:
        drawn = level_of(stream_key, extent, pieces, -0.22, 0.18) * drawn
    return jnp.clip(drawn, min=-bound, max=bound).astype(held_as)


def setup_inputs(seed: int = 0) -> dict:
    arg_keys = jax.random.split(jax.random.key(seed), 9)
    features = scatter_about(arg_keys[0], (TRAJ, LENGTH, D), 1.0, 6.0, ((0, 4), (1, 32)), jnp.float32)
    rewards = scatter_about(arg_keys[1], (TRAJ, LENGTH), 0.1, 0.8, ((0, 4), (1, 32)), jnp.float32)
    done_flags = plant((jax.random.randint(arg_keys[2], (TRAJ, LENGTH), 0, 1024) < 1).astype(jnp.int32), jax.random.fold_in(arg_keys[2], 1), 0, 1)
    traj_len = draw_traj_len(jax.random.fold_in(arg_keys[8], 71), 0)
    decay_rate = jnp.clip(jnp.exp(math.log(0.03) - 8.030084 * jax.random.uniform(arg_keys[4], (SECTIONS, K, D), jnp.float32) ** level_of(arg_keys[4], (SECTIONS, K, D), ((0, 2),), -0.2, 0.2)), 9.765624781721272e-06, 0.03)
    input_gain = scatter_about(arg_keys[5], (SECTIONS, K, D), 1.0, 4.0, ((0, 2),), jnp.float32)
    output_gain = scatter_about(arg_keys[6], (SECTIONS, K, D), K ** -0.5, 2.0, ((0, 2),), jnp.float32)
    value_head = scatter_about(arg_keys[7], (D,), D ** -0.5, 0.125, (), jnp.float32)
    return dict(features=features, rewards=rewards, done_flags=done_flags, traj_len=traj_len, decay_rate=decay_rate, input_gain=input_gain, output_gain=output_gain, value_head=value_head)


def section_seq(traj_in, retain, decay_rate, input_gain, output_gain):
    base_decay = jnp.exp(-decay_rate)
    scaled_gain = jnp.sqrt(-jnp.expm1(-2.0 * decay_rate)) * input_gain

    def advance(carried, inputs):
        token_in, retain_now = inputs
        carried = retain_now * base_decay * carried + scaled_gain * token_in[None, :]
        return (carried, lax.optimization_barrier(jnp.sum(output_gain * carried, axis=0)))
    _, ema_sum = lax.scan(advance, jnp.zeros(decay_rate.shape, jnp.float32), (traj_in, retain))
    return traj_in + jax.nn.silu(ema_sum)

def reference(features, rewards, done_flags, traj_len, decay_rate, input_gain, output_gain, value_head):
    gamma_step = math.exp(-0.25 / LENGTH)
    trace_step = math.exp(-1.0 / LENGTH)
    positions = jnp.arange(LENGTH)
    lower_list = []
    upper_list = []
    beta_lower = jnp.zeros(input_gain.shape[1:], jnp.float32)
    beta_upper = jnp.zeros(input_gain.shape[1:], jnp.float32)
    eta_lower = jnp.zeros(input_gain.shape[1:], jnp.float32)
    eta_upper = jnp.zeros(input_gain.shape[1:], jnp.float32)
    for traj_index in range(TRAJ):
        flags_row = done_flags[traj_index].astype(jnp.float32)
        retain = 1.0 - 0.5 * flags_row

        def lower_part(traj_in, gain_in, gain_out):
            return section_seq(traj_in, retain, decay_rate[0], gain_in, gain_out)

        def upper_part(traj_in, gain_in, gain_out):
            top_out = section_seq(traj_in, retain, decay_rate[1], gain_in, gain_out)
            return jnp.dot(top_out, value_head, precision=lax.Precision.HIGHEST)
        hidden, lower_vjp = jax.vjp(lower_part, features[traj_index], input_gain[0], output_gain[0])
        values, upper_vjp = jax.vjp(upper_part, hidden, input_gain[1], output_gain[1])
        valid_mask = (positions < traj_len[traj_index]).astype(jnp.float32)
        masked = values * valid_mask
        following = jnp.concatenate([masked[1:], jnp.zeros((1,), jnp.float32)])
        alive_mask = 1.0 - flags_row
        td_error = valid_mask * (rewards[traj_index] + gamma_step * alive_mask * following - values)

        def backward_step(carried, inputs):
            error_now, factor_now = inputs
            carried = error_now + factor_now * carried
            return (carried, carried)
        _, advantages = lax.scan(backward_step, jnp.zeros((), jnp.float32), (td_error, trace_step * alive_mask), reverse=True)
        grad_hidden, grad_in_up, grad_out_up = upper_vjp(-advantages * valid_mask)
        grad_features, grad_in_low, grad_out_low = lower_vjp(grad_hidden)
        lower_list.append(grad_features)
        upper_list.append(grad_hidden)
        beta_lower = beta_lower + grad_in_low
        beta_upper = beta_upper + grad_in_up
        eta_lower = eta_lower + grad_out_low
        eta_upper = eta_upper + grad_out_up
    section_input_grad = jnp.stack([jnp.stack(lower_list), jnp.stack(upper_list)])
    grad_input_gain = jnp.stack([beta_lower, beta_upper])
    grad_output_gain = jnp.stack([eta_lower, eta_upper])
    return (section_input_grad, grad_input_gain, grad_output_gain)
```

```python
import math

import jax
import jax.numpy as jnp
from jax import lax
from jax.experimental import pallas as pl
from jax.experimental.pallas import tpu as pltpu
from jax.sharding import PartitionSpec as P

F32 = jnp.float32
LANES = 128
K = 8
HALF = 64
CHUNK = 32
BLOCKS = 32
VMEM_LIMIT = 48 * 1024 * 1024


def lane_index(shape):
    return lax.broadcasted_iota(jnp.int32, shape, len(shape) - 1)


def lower_lanes(shape):
    return lane_index(shape) < HALF


def swap_halves(a):
    return pltpu.roll(a, HALF, 1)


def sigmoid(v):
    return 1.0 / (1.0 + jnp.exp(-v))


def rows_of(ref, start, stride, size=8):
    return ref[pl.ds(start, size, stride=stride), :]


def pack_kernel(feat_ref, flag_ref, p_ref, beta_ref, eta_ref, out_ref, par_ref):
    core = lax.axis_index("sect")
    lo = lower_lanes((8, LANES))
    for pair in range(BLOCKS // 2):
        for g in range(CHUNK // 8):
            early = feat_ref[0, 8 * g : 8 * g + 8, pair * LANES : (pair + 1) * LANES]
            late = feat_ref[0, CHUNK + 8 * g : CHUNK + 8 * g + 8, pair * LANES : (pair + 1) * LANES]
            even_row = 2 * pair * (CHUNK + 1) + 8 * g
            odd_row = (2 * pair + 1) * (CHUNK + 1) + 8 * g
            out_ref[even_row : even_row + 8, :] = jnp.where(lo, early, swap_halves(late))
            out_ref[odd_row : odd_row + 8, :] = jnp.where(lo, swap_halves(early), late)
    flags = flag_ref[pl.ds(core, 1), :].astype(F32)
    row = jnp.concatenate([flags, jnp.zeros((1, HALF), F32)], axis=1)
    for block in range(BLOCKS):
        at = block * (CHUNK + 1) + CHUNK
        out_ref[at : at + 1, :] = row
    p = p_ref[...]
    scale = jnp.sqrt(p * (2.0 - p))
    in_scale = scale * beta_ref[...]
    par_ref[0:8, :] = 1.0 - p
    par_ref[8:16, :] = in_scale * eta_ref[...]
    par_ref[16:24, :] = scale * eta_ref[...]
    par_ref[24:32, :] = in_scale


def channel_tile(ref, place, lo_row, rows):
    start = pl.multiple_of((place // 2) * LANES, LANES)
    tile = ref[lo_row : lo_row + rows, pl.ds(start, LANES)]
    flipped = swap_halves(tile)
    lo = lower_lanes((rows, LANES))
    odd = (place % 2) == 1
    return jnp.where(odd, jnp.where(lo, flipped, tile), jnp.where(lo, tile, flipped))


def section_params(own_ref, other_ref, core, place):
    own_q, own_w = channel_tile(own_ref, place, 0, 8), channel_tile(own_ref, place, 8, 8)
    oth_q, oth_w = channel_tile(other_ref, place, 0, 8), channel_tile(other_ref, place, 8, 8)
    first = core == 0
    return (
        (jnp.where(first, own_q, oth_q), jnp.where(first, own_w, oth_w)),
        (jnp.where(first, oth_q, own_q), jnp.where(first, oth_w, own_w)),
    )


def power32(q):
    for _ in range(5):
        q = q * q
    return q


def spread(a, k):
    return jnp.broadcast_to(a[k : k + 1, :], (8, LANES))


def ends_pass(lifted_ref, q, store_end):
    qs = [spread(q, k) for k in range(K)]
    for pair in range(2):
        groups = (2 * pair, 2 * pair + 1)

        def step(it, state):
            state = list(state)
            for u in range(4):
                r = it * 4 + u
                for i, g in enumerate(groups):
                    lifted = lifted_ref[pl.ds(pl.multiple_of(r * 32 + 8 * g, 8), 8), :]
                    for k in range(K):
                        state[i * K + k] = state[i * K + k] * qs[k] + lifted
            return tuple(state)

        state = lax.fori_loop(0, CHUNK // 4, step, tuple(jnp.zeros((8, LANES), F32) for _ in range(16)))
        for i, g in enumerate(groups):
            for k in range(K):
                store_end(k, g, state[i * K + k])


def halves_of(a):
    flipped = swap_halves(a)
    lo = lower_lanes(a.shape)
    return jnp.where(lo, a, flipped), jnp.where(lo, flipped, a)


def forward_carries(end_ref, fall_ref, q32, carry_ref, in_ref):
    lo = lower_lanes((8, LANES))
    q64 = q32 * q32
    carry = jnp.zeros((8, LANES), F32)
    for block in range(BLOCKS):
        end_early, end_late = halves_of(rows_of(end_ref, block, 32))
        fall_early, fall_late = halves_of(fall_ref[block : block + 1, :])
        entering_late = q32 * fall_early * carry + end_early
        carry_ref[block * 8 : block * 8 + 8, :] = carry
        in_ref[pl.ds(block, 8, stride=32), :] = jnp.where(lo, carry, entering_late)
        block_end = q32 * fall_late * end_early + end_late
        carry = q64 * (fall_early * fall_late) * carry + block_end


def forward_pass(lifted_ref, fall_ref, in_ref, q, w, ema_ref):
    qs = [spread(q, k) for k in range(K)]
    ws = [spread(w, k) for k in range(K)]
    for pair in range(2):
        groups = (2 * pair, 2 * pair + 1)

        def step(it, state):
            state = list(state)
            for u in range(4):
                r = it * 4 + u
                for i, g in enumerate(groups):
                    at = pl.ds(pl.multiple_of(r * 32 + 8 * g, 8), 8)
                    lifted = lifted_ref[at, :]
                    total = None
                    for k in range(K):
                        new = state[i * K + k] * qs[k] + lifted
                        state[i * K + k] = new
                        term = new * ws[k]
                        total = term if total is None else total + term
                    ema_ref[at, :] = total * fall_ref[at, :]
            return tuple(state)

        start = tuple(in_ref[k * 32 + 8 * g : k * 32 + 8 * g + 8, :] for g in groups for k in range(K))
        lax.fori_loop(0, CHUNK // 4, step, start)


def lane_sums(vectors):
    lane = lane_index((8, LANES))
    for bit in range(5):
        s = 1 << bit
        mask = (lane & s) == 0
        vectors = [
            jnp.where(
                mask,
                vectors[2 * m] + pltpu.roll(vectors[2 * m], LANES - s, 1),
                vectors[2 * m + 1] + pltpu.roll(vectors[2 * m + 1], s, 1),
            )
            for m in range(len(vectors) // 2)
        ]
    v = vectors[0]
    v = v + jnp.where((lane & 32) == 0, pltpu.roll(v, LANES - 32, 1), pltpu.roll(v, 32, 1))
    return jnp.where(lane < CHUNK, v, pltpu.roll(v, LANES - 32, 1))


def forward_kernel(
    lens_ref,
    recv_ref,
    own_ref,
    other_ref,
    head_ref,
    rewards_ref,
    td_ref,
    rise_ref,
    lift0_ref,
    lift1_ref,
    slope0_ref,
    slope1_ref,
    end0_ref,
    carry0_ref,
    carry1_ref,
    flags_ref,
    falls_ref,
    fall_ref,
    ema_ref,
    hid_ref,
    in_ref,
    end1_ref,
):
    core, place, dp = lax.axis_index("sect"), lax.axis_index("ctx"), lax.axis_index("dp")
    stride = CHUNK + 1
    (q0, w0), (q1, w1) = section_params(own_ref, other_ref, core, place)
    lo = lower_lanes((8, LANES))
    for g in range(4):
        flags = rows_of(recv_ref, 8 * g * stride + CHUNK, stride)
        flags_ref[8 * g : 8 * g + 8, :] = flags
        rise = jnp.ones((8, LANES), F32)
        fall = jnp.ones((8, LANES), F32)
        for r in range(CHUNK):
            early = jnp.broadcast_to(flags[:, r : r + 1], (8, LANES))
            late = jnp.broadcast_to(flags[:, CHUNK + r : CHUNK + r + 1], (8, LANES))
            flag = jnp.where(lo, early, late)
            rise = rise * (1.0 + flag)
            fall = fall * (1.0 - 0.5 * flag)
            at = slice(r * 32 + 8 * g, r * 32 + 8 * g + 8)
            rise_ref[at, :] = rise
            fall_ref[at, :] = fall
            lift0_ref[at, :] = rows_of(recv_ref, 8 * g * stride + r, stride) * rise
        falls_ref[8 * g : 8 * g + 8, :] = fall

    def store0(k, g, u):
        at = slice(k * 32 + 8 * g, k * 32 + 8 * g + 8)
        end0_ref[at, :] = u * falls_ref[8 * g : 8 * g + 8, :]

    def store1(k, g, u):
        at = slice(k * 32 + 8 * g, k * 32 + 8 * g + 8)
        end1_ref[at, :] = u * falls_ref[8 * g : 8 * g + 8, :]

    ends_pass(lift0_ref, q0, store0)
    forward_carries(end0_ref, falls_ref, power32(q0), carry0_ref, in_ref)
    forward_pass(lift0_ref, fall_ref, in_ref, q0, w0, ema_ref)

    def after0(it, _):
        for u in range(8):
            at = pl.ds(pl.multiple_of(it * 64 + 8 * u, 8), 8)
            ema, fall, rise = ema_ref[at, :], fall_ref[at, :], rise_ref[at, :]
            sig = sigmoid(ema)
            hidden = lift0_ref[at, :] * fall + ema * sig
            hid_ref[at, :] = hidden
            lift1_ref[at, :] = hidden * rise
            slope0_ref[at, :] = sig * (1.0 + ema * (1.0 - sig)) * fall
        return 0

    lax.fori_loop(0, 16, after0, 0)
    ends_pass(lift1_ref, q1, store1)
    forward_carries(end1_ref, falls_ref, power32(q1), carry1_ref, in_ref)
    forward_pass(lift1_ref, fall_ref, in_ref, q1, w1, ema_ref)
    start = pl.multiple_of((place // 2) * LANES, LANES)
    tile = head_ref[:, pl.ds(start, LANES)]
    flipped = swap_halves(tile)
    lo1 = lower_lanes((1, LANES))
    head = jnp.where((place % 2) == 1, jnp.where(lo1, flipped, tile), jnp.where(lo1, tile, flipped))
    head8 = jnp.broadcast_to(head, (8, LANES))

    def after1(it, _):
        for u in range(8):
            at = pl.ds(pl.multiple_of(it * 64 + 8 * u, 8), 8)
            ema = ema_ref[at, :]
            sig = sigmoid(ema)
            slope1_ref[at, :] = sig * (1.0 + ema * (1.0 - sig)) * fall_ref[at, :]
            hid_ref[at, :] = (hid_ref[at, :] + ema * sig) * head8
        return 0

    lax.fori_loop(0, 16, after1, 0)
    values = jnp.concatenate(
        [
            lane_sums([hid_ref[r * 32 + 8 * g : r * 32 + 8 * g + 8, :] for r in range(CHUNK)])
            for g in range(4)
        ],
        axis=0,
    )
    length = lens_ref[dp * 2 + core]
    total = BLOCKS * HALF
    gamma = math.exp(-0.25 / total)
    shape = (BLOCKS, LANES)
    lane = lane_index(shape)
    row = lax.broadcasted_iota(jnp.int32, shape, 0)
    position = row * HALF + lane
    next_block = pltpu.roll(pltpu.roll(values, BLOCKS - 1, 0), HALF - 1, 1)
    following = jnp.where(lane == HALF - 1, next_block, pltpu.roll(values, LANES - 1, 1))
    following = jnp.where(position + 1 < length, following, 0.0)
    part = gamma * (1.0 - flags_ref[...]) * following - values
    rewards = rewards_ref[pl.ds(core, 1), :]
    rewards = jnp.concatenate([rewards, jnp.zeros((1, HALF), F32)], axis=1)
    part = part + jnp.where(row == place, rewards, 0.0)
    half_rows = BLOCKS // 2
    packed = jnp.where(
        lower_lanes((half_rows, LANES)), part[:half_rows, :], swap_halves(part[half_rows:, :])
    )
    for block in range(BLOCKS):
        td_ref[block * half_rows : (block + 1) * half_rows, :] = packed


def starts_pass(grad_ref, lift_ref, q, start_ref):
    qs = [spread(q, k) for k in range(K)]
    sums = [None] * K
    for g in range(4):

        def step(it, state):
            state = list(state)
            for u in range(4):
                r = CHUNK - 1 - (it * 4 + u)
                at = pl.ds(pl.multiple_of(r * 32 + 8 * g, 8), 8)
                grad = grad_ref[at, :]
                lifted = lift_ref[at, :]
                for k in range(K):
                    new = state[k] * qs[k] + grad
                    state[k] = new
                    state[K + k] = state[K + k] + new * lifted
            return tuple(state)

        state = lax.fori_loop(0, CHUNK // 4, step, tuple(jnp.zeros((8, LANES), F32) for _ in range(16)))
        for k in range(K):
            start_ref[k * 32 + 8 * g : k * 32 + 8 * g + 8, :] = state[k]
            sums[k] = state[K + k] if sums[k] is None else sums[k] + state[K + k]
    return jnp.concatenate([jnp.sum(s, axis=0, keepdims=True) for s in sums], axis=0)


def backward_carries(start_ref, end_ref, fall_ref, q32, carry_ref, in_ref):
    lo = lower_lanes((8, LANES))
    q64 = q32 * q32
    carry = jnp.zeros((8, LANES), F32)
    added = jnp.zeros((8, LANES), F32)
    for block in range(BLOCKS - 1, -1, -1):
        start_early, start_late = halves_of(rows_of(start_ref, block, 32))
        fall_early, fall_late = halves_of(fall_ref[block : block + 1, :])
        entering_early = q32 * fall_late * carry + start_late
        carry_ref[block * 8 : block * 8 + 8, :] = carry
        entering = jnp.where(lo, entering_early, carry)
        added = added + entering * rows_of(end_ref, block, 32)
        if in_ref is not None:
            in_ref[pl.ds(block, 8, stride=32), :] = entering * fall_ref[block : block + 1, :]
        block_start = q32 * fall_early * start_late + start_early
        carry = q64 * (fall_early * fall_late) * carry + block_start
    return added


def backward_pass(grad_ref, top_ref, rise_ref, slope_ref, in_ref, q, w, out_ref):
    qs = [spread(q, k) for k in range(K)]
    ws = [spread(w, k) for k in range(K)]
    for pair in range(2):
        groups = (2 * pair, 2 * pair + 1)

        def step(it, state):
            state = list(state)
            for u in range(4):
                r = CHUNK - 1 - (it * 4 + u)
                for i, g in enumerate(groups):
                    at = pl.ds(pl.multiple_of(r * 32 + 8 * g, 8), 8)
                    grad = grad_ref[at, :]
                    total = None
                    for k in range(K):
                        new = state[i * K + k] * qs[k] + grad
                        state[i * K + k] = new
                        term = new * ws[k]
                        total = term if total is None else total + term
                    out_ref[at, :] = (top_ref[at, :] + rise_ref[at, :] * total) * slope_ref[at, :]
            return tuple(state)

        start = tuple(in_ref[k * 32 + 8 * g : k * 32 + 8 * g + 8, :] for g in groups for k in range(K))
        lax.fori_loop(0, CHUNK // 4, step, start)


def backward_kernel(
    lens_ref,
    td_ref,
    own_ref,
    other_ref,
    head_ref,
    flags_ref,
    falls_ref,
    rise_ref,
    lift0_ref,
    lift1_ref,
    slope0_ref,
    slope1_ref,
    end0_ref,
    end1_ref,
    carry0_ref,
    carry1_ref,
    out_ref,
    sums_ref,
    grad_ref,
    top_ref,
    gs_ref,
    start_ref,
    in_ref,
    back0_ref,
    back1_ref,
    all_ref,
):
    core, place, dp = lax.axis_index("sect"), lax.axis_index("ctx"), lax.axis_index("dp")
    (q0, w0), (q1, w1) = section_params(own_ref, other_ref, core, place)
    half_rows = BLOCKS // 2
    packed = td_ref[0:half_rows, :]
    for block in range(1, BLOCKS):
        packed = packed + td_ref[block * half_rows : (block + 1) * half_rows, :]
    length = lens_ref[dp * 2 + core]
    total = BLOCKS * HALF
    trace = math.exp(-1.0 / total)
    shape = (BLOCKS, LANES)
    lane = lane_index(shape)
    row = lax.broadcasted_iota(jnp.int32, shape, 0)
    valid = (row * HALF + lane < length) & (lane < HALF)
    td = jnp.where(valid, jnp.concatenate([packed, swap_halves(packed)], axis=0), 0.0)
    reach = trace * (1.0 - flags_ref[...])
    adv = td
    for s in (1, 2, 4, 8, 16, 32):
        inside = lane + s < HALF
        adv = adv + reach * jnp.where(inside, pltpu.roll(adv, LANES - s, 1), 0.0)
        reach = reach * jnp.where(inside, pltpu.roll(reach, LANES - s, 1), 1.0)
    block_adv = jnp.broadcast_to(adv[:, 0:1], shape)
    block_reach = jnp.broadcast_to(reach[:, 0:1], shape)
    for s in (1, 2, 4, 8, 16):
        inside = row + s < BLOCKS
        block_adv = block_adv + block_reach * jnp.where(
            inside, pltpu.roll(block_adv, BLOCKS - s, 0), 0.0
        )
        block_reach = block_reach * jnp.where(
            inside, pltpu.roll(block_reach, BLOCKS - s, 0), 1.0
        )
    arriving = jnp.where(row + 1 < BLOCKS, pltpu.roll(block_adv, BLOCKS - 1, 0), 0.0)
    grad = jnp.where(valid, -(adv + reach * arriving), 0.0)
    all_ref[...] = grad
    grad_ref[...] = all_ref[pl.ds(place, 1), :]

    start = pl.multiple_of((place // 2) * LANES, LANES)
    tile = head_ref[:, pl.ds(start, LANES)]
    flipped = swap_halves(tile)
    lo1 = lower_lanes((1, LANES))
    head = jnp.where((place % 2) == 1, jnp.where(lo1, flipped, tile), jnp.where(lo1, tile, flipped))
    head8 = jnp.broadcast_to(head, (8, LANES))
    lo = lower_lanes((8, LANES))
    for g in range(4):
        rows = grad[8 * g : 8 * g + 8, :]
        for r in range(CHUNK):
            early = jnp.broadcast_to(rows[:, r : r + 1], (8, LANES))
            late = jnp.broadcast_to(rows[:, CHUNK + r : CHUNK + r + 1], (8, LANES))
            at = slice(r * 32 + 8 * g, r * 32 + 8 * g + 8)
            top = jnp.where(lo, early, late) * head8
            top_ref[at, :] = top
            gs_ref[at, :] = top * slope1_ref[at, :]

    sums1 = starts_pass(gs_ref, lift1_ref, q1, start_ref)
    added1 = backward_carries(start_ref, end1_ref, falls_ref, power32(q1), back1_ref, in_ref)
    backward_pass(gs_ref, top_ref, rise_ref, slope0_ref, in_ref, q1, w1, gs_ref)
    sums0 = starts_pass(gs_ref, lift0_ref, q0, start_ref)
    added0 = backward_carries(start_ref, end0_ref, falls_ref, power32(q0), back0_ref, None)
    full0 = sums0 + q0 * added0
    full1 = sums1 + q1 * added1
    full0 = full0 + swap_halves(full0)
    full1 = full1 + swap_halves(full1)
    first = core == 0
    sums_ref[0] = jnp.where(first, full0, full1)
    sums_ref[1] = jnp.where(first, full1, full0)
    for block in range(BLOCKS):
        at = slice(block * 8, block * 8 + 8)
        out_ref[block * 16 : block * 16 + 8, :] = jnp.where(lo, carry0_ref[at, :], carry1_ref[at, :])
        out_ref[block * 16 + 8 : block * 16 + 16, :] = jnp.where(
            lo, back1_ref[at, :], back0_ref[at, :]
        )


def local_kernel(
    flag_ref,
    grad_ref,
    feat_ref,
    carry_ref,
    own_ref,
    other_ref,
    head_ref,
    out_ref,
    ema_ref,
    hid_ref,
    slope0_ref,
    slope1_ref,
    par_ref,
):
    core = lax.axis_index("sect")
    lo = lower_lanes((16, LANES))
    par_ref[core] = own_ref[...]
    par_ref[1 - core] = other_ref[...]
    head = head_ref[...]

    def carried(k, kind):
        base = k + 8 * (kind // 2)
        even = carry_ref[pl.ds(base, 16, stride=32), :]
        odd = carry_ref[pl.ds(16 + base, 16, stride=32), :]
        if kind % 2 == 0:
            return jnp.where(lo, even, swap_halves(odd))
        return jnp.where(lo, swap_halves(even), odd)

    def params(section, which):
        return [par_ref[section, pl.ds(which * LANES + k, 16, stride=8), :] for k in range(K)]

    def token(t):
        return pl.ds((t // 8) * LANES + t % 8, 16, stride=8)

    def local(t):
        return pl.ds(pl.multiple_of(t * 16, 16), 16)

    def forward(section, read):
        qs, ws = params(section, 0), params(section, 1)

        def step(it, state):
            rise, fall, state = state[0], state[1], list(state[2:])
            for u in range(4):
                t = it * 4 + u
                flag = flag_ref[core, t].astype(F32)
                rise = rise * (1.0 + flag)
                fall = fall * (1.0 - 0.5 * flag)
                lifted = read(t) * rise
                total = None
                for k in range(K):
                    state[k] = state[k] * qs[k] + lifted
                    term = state[k] * ws[k]
                    total = term if total is None else total + term
                ema_ref[local(t), :] = total * fall
            return (rise, fall, *state)

        begin = (jnp.float32(1.0), jnp.float32(1.0), *[carried(k, section) for k in range(K)])
        end = lax.fori_loop(0, HALF // 4, step, begin)
        return end[0], end[1]

    forward(0, lambda t: feat_ref[0, token(t), :])

    def after0(it, _):
        for u in range(4):
            t = it * 4 + u
            ema = ema_ref[local(t), :]
            sig = sigmoid(ema)
            hid_ref[local(t), :] = feat_ref[0, token(t), :] + ema * sig
            slope0_ref[local(t), :] = sig * (1.0 + ema * (1.0 - sig))
        return 0

    lax.fori_loop(0, HALF // 4, after0, 0)
    rise_end, fall_end = forward(1, lambda t: hid_ref[local(t), :])

    def after1(it, _):
        for u in range(4):
            at = local(it * 4 + u)
            ema = ema_ref[at, :]
            sig = sigmoid(ema)
            slope1_ref[at, :] = sig * (1.0 + ema * (1.0 - sig))
        return 0

    lax.fori_loop(0, HALF // 4, after1, 0)

    def backward(section, kind, read, slope_ref, slot, keep):
        qs, ws = params(section, 0), params(section, 1)

        def step(it, state):
            rise, fall, state = state[0], state[1], list(state[2:])
            for u in range(4):
                t = HALF - 1 - (it * 4 + u)
                flag = flag_ref[core, t].astype(F32)
                grad_out = read(t)
                lifted = grad_out * slope_ref[local(t), :] * fall
                total = None
                for k in range(K):
                    state[k] = state[k] * qs[k] + lifted
                    term = state[k] * ws[k]
                    total = term if total is None else total + term
                grad_in = grad_out + total * rise
                out_ref[slot, token(t), :] = grad_in
                if keep:
                    hid_ref[local(t), :] = grad_in
                rise = rise * (1.0 - 0.5 * flag)
                fall = fall * (1.0 + flag)
            return (rise, fall, *state)

        begin = (rise_end, fall_end, *[carried(k, kind) * fall_end for k in range(K)])
        lax.fori_loop(0, HALF // 4, step, begin)

    backward(1, 2, lambda t: head * grad_ref[0, t], slope1_ref, 1 - core, True)
    backward(0, 3, lambda t: hid_ref[local(t), :], slope0_ref, core, False)


def vmem():
    return pl.BlockSpec(memory_space=pltpu.VMEM)


def smem():
    return pl.BlockSpec(memory_space=pltpu.SMEM)


def compiler_params():
    return pltpu.CompilerParams(vmem_limit_bytes=VMEM_LIMIT)


def shape_of(*dims):
    return jax.ShapeDtypeStruct(dims, F32)


def scratch(*dims):
    return pltpu.VMEM(dims, F32)


def tiles(a):
    rows, width = a.shape
    return (
        a.reshape(rows // 8, 8, width // LANES, LANES)
        .transpose(0, 2, 1, 3)
        .reshape(rows * width // LANES, LANES)
    )


def per_device(
    features, rewards, done_flags, traj_len, decay_rate, input_gain, output_gain, value_head
):
    micro_rows, steps_local, width = features.shape
    core = lax.axis_index("sect")
    place = lax.axis_index("ctx")
    rows = CHUNK * BLOCKS
    shrink = -jnp.expm1(-decay_rate[0])
    sent, params = pl.pallas_call(
        pack_kernel,
        grid=(1,),
        in_specs=[
            pl.BlockSpec((1, steps_local, width), lambda i: (lax.axis_index("sect"), 0, 0)),
            vmem(),
            vmem(),
            vmem(),
            vmem(),
        ],
        out_specs=[vmem(), vmem()],
        out_shape=[shape_of(BLOCKS * (CHUNK + 1), LANES), shape_of(4 * K, width)],
        compiler_params=compiler_params(),
        name="pack",
    )(features, done_flags, shrink, input_gain[0], output_gain[0])
    own = params[: 2 * K]
    other = lax.ppermute(own, "sect", [(0, 1), (1, 0)])
    received = lax.all_to_all(sent.reshape(BLOCKS, CHUNK + 1, 1, LANES), "ctx", 0, 0).reshape(
        BLOCKS * (CHUNK + 1), LANES
    )
    head = value_head.reshape(1, width)
    half_rows = BLOCKS // 2
    td_parts, rise, lift0, lift1, slope0, slope1, end0, carry0, carry1, flags, falls, end1 = (
        pl.pallas_call(
            lambda *refs: forward_kernel(*refs[:17], *refs[18:22], refs[17]),
            in_specs=[smem(), vmem(), vmem(), vmem(), vmem(), vmem()],
            out_specs=[vmem()] * 12,
            out_shape=[shape_of(BLOCKS * half_rows, LANES)]
            + [shape_of(rows, LANES)] * 5
            + [shape_of(K * 32, LANES)] * 3
            + [shape_of(BLOCKS, LANES)] * 2
            + [shape_of(K * 32, LANES)],
            scratch_shapes=[
                scratch(rows, LANES),
                scratch(rows, LANES),
                scratch(rows, LANES),
                scratch(K * 32, LANES),
            ],
            compiler_params=compiler_params(),
            name="forward",
        )(traj_len, received, own, other, head, rewards)
    )
    td_all = lax.all_to_all(td_parts.reshape(BLOCKS, half_rows, LANES), "ctx", 0, 0).reshape(
        BLOCKS * half_rows, LANES
    )
    carries, sums, grad_values = pl.pallas_call(
        backward_kernel,
        in_specs=[smem()] + [vmem()] * 15,
        out_specs=[vmem()] * 3,
        out_shape=[shape_of(BLOCKS * 16, LANES), shape_of(2, K, LANES), shape_of(1, LANES)],
        scratch_shapes=[
            scratch(rows, LANES),
            scratch(rows, LANES),
            scratch(K * 32, LANES),
            scratch(K * 32, LANES),
            scratch(K * 32, LANES),
            scratch(K * 32, LANES),
            scratch(BLOCKS, LANES),
        ],
        compiler_params=compiler_params(),
        name="backward",
    )(
        traj_len,
        td_all,
        own,
        other,
        head,
        flags,
        falls,
        rise,
        lift0,
        lift1,
        slope0,
        slope1,
        end0,
        end1,
        carry0,
        carry1,
    )
    from_core = lax.ppermute(sums[1], "sect", [(0, 1), (1, 0)])
    carries = lax.all_to_all(carries.reshape(BLOCKS, 16, LANES), "ctx", 0, 0).reshape(
        BLOCKS * 16, LANES
    )
    total = sums[0] + from_core
    total = total + lax.ppermute(total, "dp", [(0, 1), (1, 0), (2, 3), (3, 2)])
    total = total + lax.ppermute(total, "dp", [(0, 2), (1, 3), (2, 0), (3, 1)])
    gains = lax.dynamic_slice(params, (2 * K, place * HALF), (2 * K, HALF))
    grad_gains = gains * jnp.concatenate([total[:, :HALF], total[:, :HALF]], axis=0)

    grads = pl.pallas_call(
        local_kernel,
        grid=(1,),
        in_specs=[
            smem(),
            smem(),
            pl.BlockSpec((1, rows, LANES), lambda i: (lax.axis_index("sect"), 0, 0)),
            vmem(),
            vmem(),
            vmem(),
            vmem(),
        ],
        out_specs=vmem(),
        out_shape=shape_of(2, rows, LANES),
        scratch_shapes=[
            scratch(rows, LANES),
            scratch(rows, LANES),
            scratch(rows, LANES),
            scratch(rows, LANES),
            scratch(2, 2 * LANES, LANES),
        ],
        compiler_params=compiler_params(),
        name="local",
    )(
        done_flags,
        grad_values,
        jnp.stack([tiles(features[0]), tiles(features[1])]),
        carries,
        tiles(own),
        tiles(other),
        head.reshape(width // LANES, LANES),
    )
    swapped = lax.ppermute(grads[1], "sect", [(0, 1), (1, 0)])
    mine = grads[0]
    both = jnp.stack([jnp.where(core == 0, mine, swapped), jnp.where(core == 0, swapped, mine)])
    grad_inputs = (
        both.reshape(2, steps_local // 8, width // LANES, 8, LANES)
        .transpose(0, 1, 3, 2, 4)
        .reshape(1, micro_rows, steps_local, width)
    )
    return (grad_inputs, grad_gains[None, :K], grad_gains[None, K:])


def solution(mesh):
    placed = (
        P("dp", "ctx", None),
        P("dp", "ctx"),
        P("dp", "ctx"),
        P(),
        P("sect", None, None),
        P("sect", None, None),
        P("sect", None, None),
        P(),
    )
    return jax.shard_map(
        per_device,
        mesh=mesh,
        in_specs=placed,
        out_specs=(P("sect", "dp", "ctx", None), P("sect", None, "ctx"), P("sect", None, "ctx")),
        check_vma=False,
    )
```

```python
import math

import jax
import jax.numpy as jnp
from jax import lax
from jax.experimental import pallas as pl
from jax.experimental.pallas import tpu as pltpu
from jax.sharding import PartitionSpec as P

F32 = jnp.float32
LANES = 128
K = 8
HALF = 64
CHUNK = 32
BLOCKS = 32
VMEM_LIMIT = 12 * 1024 * 1024
AUX_ROWS = 64


def lane_index(shape):
    return lax.broadcasted_iota(jnp.int32, shape, len(shape) - 1)


def lower_lanes(shape):
    return lane_index(shape) < HALF


def swap_halves(a):
    return pltpu.roll(a, HALF, 1)


def sigmoid(v):
    return 1.0 / (1.0 + jnp.exp(-v))


def rows_of(ref, start, stride, size=8):
    return ref[pl.ds(start, size, stride=stride), :]


def pack_kernel(feat_hbm, flag_hbm, out_ref, feat_ref, flag_ref, sems):
    core = lax.axis_index("sect")

    def piece(i):
        at = pl.ds(8 * i, 8)
        return pltpu.make_async_copy(feat_hbm.at[core, at], feat_ref.at[at], sems.at[i])

    flag_copy = pltpu.make_async_copy(flag_hbm, flag_ref, sems.at[8])
    for g in range(4):
        piece(g).start()
        piece(g + 4).start()
    flag_copy.start()
    lo = lower_lanes((8, LANES))
    for g in range(CHUNK // 8):
        piece(g).wait()
        piece(g + 4).wait()
        for pair in range(BLOCKS // 2):
            early = feat_ref[8 * g : 8 * g + 8, pair * LANES : (pair + 1) * LANES]
            late = feat_ref[CHUNK + 8 * g : CHUNK + 8 * g + 8, pair * LANES : (pair + 1) * LANES]
            even_row = 2 * pair * (CHUNK + 1) + 8 * g
            odd_row = (2 * pair + 1) * (CHUNK + 1) + 8 * g
            out_ref[even_row : even_row + 8, :] = jnp.where(lo, early, swap_halves(late))
            out_ref[odd_row : odd_row + 8, :] = jnp.where(lo, swap_halves(early), late)
    flag_copy.wait()
    flags = flag_ref[pl.ds(core, 1), :].astype(F32)
    row = jnp.concatenate([flags, jnp.zeros((1, HALF), F32)], axis=1)
    for block in range(BLOCKS):
        at = block * (CHUNK + 1) + CHUNK
        out_ref[at : at + 1, :] = row


def rates_kernel(p_ref, beta_ref, eta_ref, own_ref, gain_ref):
    p = p_ref[...]
    scale = jnp.sqrt(p * (2.0 - p))
    in_scale = scale * beta_ref[...]
    own_ref[0:8, :] = 1.0 - p
    own_ref[8:16, :] = in_scale * eta_ref[...]
    gain_ref[0:8, :] = scale * eta_ref[...]
    gain_ref[8:16, :] = in_scale


def channel_tile(ref, place, lo_row, rows):
    start = pl.multiple_of((place // 2) * LANES, LANES)
    tile = ref[lo_row : lo_row + rows, pl.ds(start, LANES)]
    flipped = swap_halves(tile)
    lo = lower_lanes((rows, LANES))
    odd = (place % 2) == 1
    return jnp.where(odd, jnp.where(lo, flipped, tile), jnp.where(lo, tile, flipped))


def tables_kernel(
    lens_ref,
    flag_ref,
    own_ref,
    other_ref,
    gain_ref,
    head_ref,
    rewards_ref,
    aux_ref,
    par_ref,
    scale_ref,
    power_ref,
):
    core, place, dp = lax.axis_index("sect"), lax.axis_index("ctx"), lax.axis_index("dp")
    for section in range(2):
        here = core == section
        q = jnp.where(here, channel_tile(own_ref, place, 0, 8), channel_tile(other_ref, place, 0, 8))
        w = jnp.where(here, channel_tile(own_ref, place, 8, 8), channel_tile(other_ref, place, 8, 8))
        aux_ref[16 * section : 16 * section + 8, :] = q
        aux_ref[16 * section + 8 : 16 * section + 16, :] = w
        aux_ref[32 + 8 * section : 40 + 8 * section, :] = power32(q)
        for which in range(2):
            for tile in range(16):
                rows, lanes = slice(8 * which, 8 * which + 8), slice(tile * LANES, (tile + 1) * LANES)
                at = which * LANES + tile * 8
                par_ref[section, at : at + 8, :] = jnp.where(here, own_ref[rows, lanes], other_ref[rows, lanes])
    aux_ref[48:56, :] = jnp.broadcast_to(channel_tile(head_ref, place, 0, 1), (8, LANES))
    rewards = rewards_ref[pl.ds(core, 1), :]
    aux_ref[56:57, :] = jnp.concatenate([rewards, jnp.zeros((1, HALF), F32)], axis=1)
    aux_ref[57:64, :] = jnp.full((7, LANES), lens_ref[dp * 2 + core].astype(F32))
    scale_ref[...] = channel_tile(gain_ref, place, 0, 16)
    rise = jnp.float32(1.0)
    fall = jnp.float32(1.0)
    for t in range(HALF):
        flag = flag_ref[core, t].astype(F32)
        rise = rise * (1.0 + flag)
        fall = fall * (1.0 - 0.5 * flag)
        power_ref[t : t + 1, :] = jnp.full((1, LANES), rise)
        power_ref[HALF + t : HALF + t + 1, :] = jnp.full((1, LANES), fall)


def power32(q):
    for _ in range(5):
        q = q * q
    return q


def spread(a, k):
    return jnp.broadcast_to(a[k : k + 1, :], (8, LANES))


def ends_pass(lifted_ref, q, store_end):
    qs = [spread(q, k) for k in range(K)]
    for pair in range(2):
        groups = (2 * pair, 2 * pair + 1)

        def step(it, state):
            state = list(state)
            for u in range(4):
                r = it * 4 + u
                for i, g in enumerate(groups):
                    lifted = lifted_ref[pl.ds(pl.multiple_of(r * 32 + 8 * g, 8), 8), :]
                    for k in range(K):
                        state[i * K + k] = state[i * K + k] * qs[k] + lifted
            return tuple(state)

        state = lax.fori_loop(0, CHUNK // 4, step, tuple(jnp.zeros((8, LANES), F32) for _ in range(16)))
        for i, g in enumerate(groups):
            for k in range(K):
                store_end(k, g, state[i * K + k])


def halves_of(a):
    flipped = swap_halves(a)
    lo = lower_lanes(a.shape)
    return jnp.where(lo, a, flipped), jnp.where(lo, flipped, a)


def forward_carries(end_ref, fall_ref, q32, carry_ref, in_ref):
    lo = lower_lanes((8, LANES))
    q64 = q32 * q32
    carry = jnp.zeros((8, LANES), F32)
    for block in range(BLOCKS):
        end_early, end_late = halves_of(rows_of(end_ref, block, 32))
        fall_early, fall_late = halves_of(fall_ref[block : block + 1, :])
        entering_late = q32 * fall_early * carry + end_early
        carry_ref[block * 8 : block * 8 + 8, :] = carry
        in_ref[pl.ds(block, 8, stride=32), :] = jnp.where(lo, carry, entering_late)
        block_end = q32 * fall_late * end_early + end_late
        carry = q64 * (fall_early * fall_late) * carry + block_end


def forward_pass(lifted_ref, fall_ref, in_ref, q, w, ema_ref):
    qs = [spread(q, k) for k in range(K)]
    ws = [spread(w, k) for k in range(K)]
    for pair in range(2):
        groups = (2 * pair, 2 * pair + 1)

        def step(it, state):
            state = list(state)
            for u in range(4):
                r = it * 4 + u
                for i, g in enumerate(groups):
                    at = pl.ds(pl.multiple_of(r * 32 + 8 * g, 8), 8)
                    lifted = lifted_ref[at, :]
                    total = None
                    for k in range(K):
                        new = state[i * K + k] * qs[k] + lifted
                        state[i * K + k] = new
                        term = new * ws[k]
                        total = term if total is None else total + term
                    ema_ref[at, :] = total * fall_ref[at, :]
            return tuple(state)

        start = tuple(in_ref[k * 32 + 8 * g : k * 32 + 8 * g + 8, :] for g in groups for k in range(K))
        lax.fori_loop(0, CHUNK // 4, step, start)


def lane_sums(vectors):
    lane = lane_index((8, LANES))
    for bit in range(5):
        s = 1 << bit
        mask = (lane & s) == 0
        vectors = [
            jnp.where(
                mask,
                vectors[2 * m] + pltpu.roll(vectors[2 * m], LANES - s, 1),
                vectors[2 * m + 1] + pltpu.roll(vectors[2 * m + 1], s, 1),
            )
            for m in range(len(vectors) // 2)
        ]
    v = vectors[0]
    v = v + jnp.where((lane & 32) == 0, pltpu.roll(v, LANES - 32, 1), pltpu.roll(v, 32, 1))
    return jnp.where(lane < CHUNK, v, pltpu.roll(v, LANES - 32, 1))


PAYLOAD = BLOCKS // 2 + K


def forward_kernel(
    recv_ref,
    aux_ref,
    out_ref,
    lift0_ref,
    lift1_ref,
    slope0_ref,
    slope1_ref,
    end0_ref,
    flags_ref,
    falls_ref,
    rise_ref,
    fall_ref,
    ema_ref,
    hid_ref,
    end1_ref,
    in_ref,
    carry0_ref,
    carry1_ref,
):
    place = lax.axis_index("ctx")
    stride = CHUNK + 1
    q0, w0, q1, w1 = (aux_ref[8 * i : 8 * i + 8, :] for i in range(4))
    lo = lower_lanes((8, LANES))
    for g in range(4):
        flags = rows_of(recv_ref, 8 * g * stride + CHUNK, stride)
        flags_ref[8 * g : 8 * g + 8, :] = flags
        rise = jnp.ones((8, LANES), F32)
        fall = jnp.ones((8, LANES), F32)
        for r in range(CHUNK):
            early = jnp.broadcast_to(flags[:, r : r + 1], (8, LANES))
            late = jnp.broadcast_to(flags[:, CHUNK + r : CHUNK + r + 1], (8, LANES))
            flag = jnp.where(lo, early, late)
            rise = rise * (1.0 + flag)
            fall = fall * (1.0 - 0.5 * flag)
            at = slice(r * 32 + 8 * g, r * 32 + 8 * g + 8)
            rise_ref[at, :] = rise
            fall_ref[at, :] = fall
            lift0_ref[at, :] = rows_of(recv_ref, 8 * g * stride + r, stride) * rise
        falls_ref[8 * g : 8 * g + 8, :] = fall

    def store(end_ref):
        def one(k, g, u):
            at = slice(k * 32 + 8 * g, k * 32 + 8 * g + 8)
            end_ref[at, :] = u * falls_ref[8 * g : 8 * g + 8, :]

        return one

    ends_pass(lift0_ref, q0, store(end0_ref))
    forward_carries(end0_ref, falls_ref, aux_ref[32:40, :], carry0_ref, in_ref)
    forward_pass(lift0_ref, fall_ref, in_ref, q0, w0, ema_ref)

    def after0(it, _):
        for u in range(8):
            at = pl.ds(pl.multiple_of(it * 64 + 8 * u, 8), 8)
            ema, fall = ema_ref[at, :], fall_ref[at, :]
            sig = sigmoid(ema)
            hidden = lift0_ref[at, :] * fall + ema * sig
            hid_ref[at, :] = hidden
            lift1_ref[at, :] = hidden * rise_ref[at, :]
            slope0_ref[at, :] = sig * (1.0 + ema * (1.0 - sig)) * fall
        return 0

    lax.fori_loop(0, 16, after0, 0)
    ends_pass(lift1_ref, q1, store(end1_ref))
    forward_carries(end1_ref, falls_ref, aux_ref[40:48, :], carry1_ref, in_ref)
    forward_pass(lift1_ref, fall_ref, in_ref, q1, w1, ema_ref)
    head8 = aux_ref[48:56, :]

    def after1(it, _):
        for u in range(8):
            at = pl.ds(pl.multiple_of(it * 64 + 8 * u, 8), 8)
            ema = ema_ref[at, :]
            sig = sigmoid(ema)
            slope1_ref[at, :] = sig * (1.0 + ema * (1.0 - sig)) * fall_ref[at, :]
            hid_ref[at, :] = (hid_ref[at, :] + ema * sig) * head8
        return 0

    lax.fori_loop(0, 16, after1, 0)
    values = jnp.concatenate(
        [
            lane_sums([hid_ref[r * 32 + 8 * g : r * 32 + 8 * g + 8, :] for r in range(CHUNK)])
            for g in range(4)
        ],
        axis=0,
    )
    total = BLOCKS * HALF
    gamma = math.exp(-0.25 / total)
    shape = (BLOCKS, LANES)
    lane = lane_index(shape)
    row = lax.broadcasted_iota(jnp.int32, shape, 0)
    after = (row * HALF + lane + 1).astype(F32)
    next_block = pltpu.roll(pltpu.roll(values, BLOCKS - 1, 0), HALF - 1, 1)
    following = jnp.where(lane == HALF - 1, next_block, pltpu.roll(values, LANES - 1, 1))
    following = jnp.where(after < aux_ref[57:58, :], following, 0.0)
    part = gamma * (1.0 - flags_ref[...]) * following - values
    part = part + jnp.where(row == place, aux_ref[56:57, :], 0.0)
    half_rows = BLOCKS // 2
    packed = jnp.where(
        lower_lanes((half_rows, LANES)), part[:half_rows, :], swap_halves(part[half_rows:, :])
    )
    for block in range(BLOCKS):
        at = block * PAYLOAD
        rows = slice(block * 8, block * 8 + 8)
        out_ref[at : at + half_rows, :] = packed
        out_ref[at + half_rows : at + PAYLOAD, :] = jnp.where(lo, carry0_ref[rows, :], carry1_ref[rows, :])


def starts_pass(grad_ref, q, start_ref, lift_ref=None):
    qs = [spread(q, k) for k in range(K)]
    sums = [jnp.zeros((8, LANES), F32) for _ in range(K)]
    for pair in range(2):
        groups = (2 * pair, 2 * pair + 1)

        def step(it, state):
            state = list(state)
            for u in range(4):
                r = CHUNK - 1 - (it * 4 + u)
                for i, g in enumerate(groups):
                    at = pl.ds(pl.multiple_of(r * 32 + 8 * g, 8), 8)
                    grad = grad_ref[at, :]
                    lifted = None if lift_ref is None else lift_ref[at, :]
                    for k in range(K):
                        new = state[i * K + k] * qs[k] + grad
                        state[i * K + k] = new
                        if lift_ref is not None:
                            state[16 + k] = state[16 + k] + new * lifted
            return tuple(state)

        begin = [jnp.zeros((8, LANES), F32) for _ in range(16)]
        if lift_ref is not None:
            begin = begin + sums
        state = lax.fori_loop(0, CHUNK // 4, step, tuple(begin))
        sums = list(state[16:])
        for i, g in enumerate(groups):
            for k in range(K):
                start_ref[k * 32 + 8 * g : k * 32 + 8 * g + 8, :] = state[i * K + k]
    return sums


def backward_carries(start_ref, fall_ref, q32, carry_ref, in_ref=None, end_ref=None):
    lo = lower_lanes((8, LANES))
    q64 = q32 * q32
    carry = jnp.zeros((8, LANES), F32)
    added = jnp.zeros((8, LANES), F32)
    for block in range(BLOCKS - 1, -1, -1):
        start_early, start_late = halves_of(rows_of(start_ref, block, 32))
        fall_early, fall_late = halves_of(fall_ref[block : block + 1, :])
        entering_early = q32 * fall_late * carry + start_late
        carry_ref[block * 8 : block * 8 + 8, :] = carry
        entering = jnp.where(lo, entering_early, carry)
        if in_ref is not None:
            in_ref[pl.ds(block, 8, stride=32), :] = entering * fall_ref[block : block + 1, :]
        if end_ref is not None:
            added = added + entering * rows_of(end_ref, block, 32)
        block_start = q32 * fall_early * start_late + start_early
        carry = q64 * (fall_early * fall_late) * carry + block_start
    return added


def backward_pass(grad_ref, top_ref, rise_ref, slope_ref, lift_ref, in_ref, q, w, out_ref):
    qs = [spread(q, k) for k in range(K)]
    ws = [spread(w, k) for k in range(K)]
    sums = [jnp.zeros((8, LANES), F32) for _ in range(K)]
    for pair in range(2):
        groups = (2 * pair, 2 * pair + 1)

        def step(it, state):
            state = list(state)
            for u in range(4):
                r = CHUNK - 1 - (it * 4 + u)
                for i, g in enumerate(groups):
                    at = pl.ds(pl.multiple_of(r * 32 + 8 * g, 8), 8)
                    grad = grad_ref[at, :]
                    lifted = lift_ref[at, :]
                    total = None
                    for k in range(K):
                        new = state[i * K + k] * qs[k] + grad
                        state[i * K + k] = new
                        state[16 + k] = state[16 + k] + new * lifted
                        term = new * ws[k]
                        total = term if total is None else total + term
                    out_ref[at, :] = (top_ref[at, :] + rise_ref[at, :] * total) * slope_ref[at, :]
            return tuple(state)

        start = [in_ref[k * 32 + 8 * g : k * 32 + 8 * g + 8, :] for g in groups for k in range(K)]
        state = lax.fori_loop(0, CHUNK // 4, step, tuple(start + sums))
        sums = list(state[16:])
    return sums


def folded(sums):
    return jnp.concatenate([jnp.sum(a, axis=0, keepdims=True) for a in sums], axis=0)


def backward_kernel(
    td_ref,
    aux_ref,
    flags_ref,
    falls_ref,
    lift0_ref,
    lift1_ref,
    slope0_ref,
    slope1_ref,
    end0_ref,
    out_hbm,
    small_ref,
    gs_ref,
    top_ref,
    rise_ref,
    start_ref,
    back0_ref,
    back1_ref,
    in_ref,
    both_ref,
    all_ref,
    sems,
):
    core, place = lax.axis_index("sect"), lax.axis_index("ctx")
    q0, w0, q1, w1 = (aux_ref[8 * i : 8 * i + 8, :] for i in range(4))
    half_rows = BLOCKS // 2
    packed = td_ref[0:half_rows, :]
    for block in range(1, BLOCKS):
        packed = packed + td_ref[block * PAYLOAD : block * PAYLOAD + half_rows, :]
    total = BLOCKS * HALF
    trace = math.exp(-1.0 / total)
    shape = (BLOCKS, LANES)
    lane = lane_index(shape)
    row = lax.broadcasted_iota(jnp.int32, shape, 0)
    valid = ((row * HALF + lane).astype(F32) < aux_ref[57:58, :]) & (lane < HALF)
    td = jnp.where(valid, jnp.concatenate([packed, swap_halves(packed)], axis=0), 0.0)
    reach = trace * (1.0 - flags_ref[...])
    adv = td
    for s in (1, 2, 4, 8, 16, 32):
        inside = lane + s < HALF
        adv = adv + reach * jnp.where(inside, pltpu.roll(adv, LANES - s, 1), 0.0)
        reach = reach * jnp.where(inside, pltpu.roll(reach, LANES - s, 1), 1.0)
    block_adv = jnp.broadcast_to(adv[:, 0:1], shape)
    block_reach = jnp.broadcast_to(reach[:, 0:1], shape)
    for s in (1, 2, 4, 8, 16):
        inside = row + s < BLOCKS
        block_adv = block_adv + block_reach * jnp.where(
            inside, pltpu.roll(block_adv, BLOCKS - s, 0), 0.0
        )
        block_reach = block_reach * jnp.where(
            inside, pltpu.roll(block_reach, BLOCKS - s, 0), 1.0
        )
    arriving = jnp.where(row + 1 < BLOCKS, pltpu.roll(block_adv, BLOCKS - 1, 0), 0.0)
    grad = jnp.where(valid, -(adv + reach * arriving), 0.0)
    all_ref[...] = grad
    small_ref[16:24, :] = jnp.broadcast_to(all_ref[pl.ds(place, 1), :], (8, LANES))

    head8 = aux_ref[48:56, :]
    lo = lower_lanes((8, LANES))
    for g in range(4):
        rows = grad[8 * g : 8 * g + 8, :]
        flags = flags_ref[8 * g : 8 * g + 8, :]
        rise = jnp.ones((8, LANES), F32)
        for r in range(CHUNK):
            at = slice(r * 32 + 8 * g, r * 32 + 8 * g + 8)
            early = jnp.broadcast_to(flags[:, r : r + 1], (8, LANES))
            late = jnp.broadcast_to(flags[:, CHUNK + r : CHUNK + r + 1], (8, LANES))
            rise = rise * (1.0 + jnp.where(lo, early, late))
            rise_ref[at, :] = rise
            early = jnp.broadcast_to(rows[:, r : r + 1], (8, LANES))
            late = jnp.broadcast_to(rows[:, CHUNK + r : CHUNK + r + 1], (8, LANES))
            top = jnp.where(lo, early, late) * head8
            top_ref[at, :] = top
            gs_ref[at, :] = top * slope1_ref[at, :]

    starts_pass(gs_ref, q1, start_ref)
    backward_carries(start_ref, falls_ref, aux_ref[40:48, :], back1_ref, in_ref)
    sums1 = backward_pass(gs_ref, top_ref, rise_ref, slope0_ref, lift1_ref, in_ref, q1, w1, gs_ref)
    sums0 = starts_pass(gs_ref, q0, start_ref, lift0_ref)
    added0 = backward_carries(start_ref, falls_ref, aux_ref[32:40, :], back0_ref, None, end0_ref)
    copies = []
    for part in range(4):
        for block in range(8 * part, 8 * part + 8):
            at = slice(block * 8, block * 8 + 8)
            both_ref[block] = jnp.where(lo, back1_ref[at, :], back0_ref[at, :])
        piece = pl.ds(8 * part, 8)
        copies.append(pltpu.make_async_copy(both_ref.at[piece], out_hbm.at[piece], sems.at[part]))
        copies[-1].start()
    full0 = folded(sums0) + q0 * added0
    full1 = folded(sums1)
    full0 = full0 + swap_halves(full0)
    full1 = full1 + swap_halves(full1)
    first = core == 0
    small_ref[0:8, :] = jnp.where(first, full0, full1)
    small_ref[8:16, :] = jnp.where(first, full1, full0)
    for copy in copies:
        copy.wait()


def carried(carry_ref, k, rows, base, upper):
    lo = lower_lanes((16, LANES))
    even = carry_ref[pl.ds(base + k, 16, stride=2 * rows), :]
    odd = carry_ref[pl.ds(rows + base + k, 16, stride=2 * rows), :]
    if upper:
        return jnp.where(lo, swap_halves(even), odd)
    return jnp.where(lo, even, swap_halves(odd))


def token(t):
    return pl.ds((t // 8) * LANES + t % 8, 16, stride=8)


def local(t):
    return pl.ds(pl.multiple_of(t * 16, 16), 16)


def section_rates(par_ref, section, which):
    return [par_ref[section, pl.ds(which * LANES + k, 16, stride=8), :] for k in range(K)]


def local_forward_kernel(
    small_ref,
    feat_ref,
    carry_ref,
    par_ref,
    power_ref,
    head_ref,
    top_ref,
    gs1_ref,
    slope0_ref,
    ema_ref,
    hid_ref,
    grad_ref,
):
    core = lax.axis_index("sect")
    head = head_ref[...]
    row = small_ref[16:17, :]
    for t in range(HALF):
        grad_ref[t : t + 1, :] = jnp.broadcast_to(row[:, t : t + 1], (1, LANES))

    def rise_at(t):
        return jnp.broadcast_to(power_ref[pl.ds(t, 1), :], (16, LANES))

    def fall_at(t):
        return jnp.broadcast_to(power_ref[pl.ds(HALF + t, 1), :], (16, LANES))

    def forward(section, read):
        qs, ws = section_rates(par_ref, section, 0), section_rates(par_ref, section, 1)

        def step(it, state):
            state = list(state)
            for u in range(4):
                t = it * 4 + u
                lifted = read(t) * rise_at(t)
                total = None
                for k in range(K):
                    state[k] = state[k] * qs[k] + lifted
                    term = state[k] * ws[k]
                    total = term if total is None else total + term
                ema_ref[local(t), :] = total * fall_at(t)
            return tuple(state)

        begin = tuple(carried(carry_ref, k, PAYLOAD, BLOCKS // 2, section == 1) for k in range(K))
        lax.fori_loop(0, HALF // 4, step, begin)

    forward(0, lambda t: feat_ref[core, token(t), :])

    def after0(it, _):
        for u in range(4):
            t = it * 4 + u
            ema = ema_ref[local(t), :]
            sig = sigmoid(ema)
            hid_ref[local(t), :] = feat_ref[core, token(t), :] + ema * sig
            slope0_ref[local(t), :] = sig * (1.0 + ema * (1.0 - sig)) * fall_at(t)
        return 0

    lax.fori_loop(0, HALF // 4, after0, 0)
    forward(1, lambda t: hid_ref[local(t), :])

    def after1(it, _):
        for u in range(4):
            t = it * 4 + u
            ema = ema_ref[local(t), :]
            sig = sigmoid(ema)
            top = head * jnp.broadcast_to(grad_ref[pl.ds(t, 1), :], (16, LANES))
            top_ref[local(t), :] = top
            gs1_ref[local(t), :] = top * (sig * (1.0 + ema * (1.0 - sig)) * fall_at(t))
        return 0

    lax.fori_loop(0, HALF // 4, after1, 0)


def local_backward_kernel(
    carry_ref,
    par_ref,
    top_ref,
    gs1_ref,
    slope0_ref,
    power_ref,
    sums_ref,
    sums1_ref,
    sums2_ref,
    sums3_ref,
    keep_ref,
    send_ref,
    mine_ref,
    gs0_ref,
    hid_ref,
):
    core = lax.axis_index("sect")
    rows = CHUNK * BLOCKS
    pick = slice(0, 16)
    total = (sums_ref[pick, :] + sums1_ref[pick, :]) + (sums2_ref[pick, :] + sums3_ref[pick, :])
    mine_ref[...] = total[0:8, :]
    send_ref[rows : rows + 8, :] = total[8:16, :]
    fall_end = jnp.broadcast_to(power_ref[2 * HALF - 1 : 2 * HALF, :], (16, LANES))

    def backward(section, read, gs_ref, finish):
        qs, ws = section_rates(par_ref, section, 0), section_rates(par_ref, section, 1)

        def step(it, state):
            state = list(state)
            for u in range(4):
                t = HALF - 1 - (it * 4 + u)
                lifted = gs_ref[local(t), :]
                total = None
                for k in range(K):
                    state[k] = state[k] * qs[k] + lifted
                    term = state[k] * ws[k]
                    total = term if total is None else total + term
                rise = jnp.broadcast_to(power_ref[pl.ds(t, 1), :], (16, LANES))
                finish(t, read(t) + total * rise)
            return tuple(state)

        begin = tuple(carried(carry_ref, k, K, 0, section == 0) * fall_end for k in range(K))
        lax.fori_loop(0, HALF // 4, step, begin)

    def run(upper_ref, lower_ref):
        def finish1(t, grad):
            upper_ref[token(t), :] = grad
            hid_ref[local(t), :] = grad
            gs0_ref[local(t), :] = grad * slope0_ref[local(t), :]

        def finish0(t, grad):
            lower_ref[token(t), :] = grad

        backward(1, lambda t: top_ref[local(t), :], gs1_ref, finish1)
        backward(0, lambda t: hid_ref[local(t), :], gs0_ref, finish0)

    @pl.when(core == 0)
    def _():
        run(send_ref, keep_ref)

    @pl.when(core == 1)
    def _():
        run(keep_ref, send_ref)


def place_kernel(keep_ref, out_hbm, sems):
    core = lax.axis_index("sect")
    copies = [
        pltpu.make_async_copy(
            keep_ref.at[pl.ds(i * 256, 256)], out_hbm.at[core, pl.ds(i * 256, 256)], sems.at[i]
        )
        for i in range(4)
    ]
    for copy in copies:
        copy.start()
    for copy in copies:
        copy.wait()


def finish_kernel(
    recv_ref, mine_ref, scale_ref, placed_hbm, out_hbm, beta_hbm, eta_hbm, beta_ref, eta_ref, sems
):
    del placed_hbm
    core = lax.axis_index("sect")
    rows = CHUNK * BLOCKS
    copies = [
        pltpu.make_async_copy(
            recv_ref.at[pl.ds(i * 256, 256)], out_hbm.at[1 - core, pl.ds(i * 256, 256)], sems.at[i]
        )
        for i in range(4)
    ]
    for copy in copies:
        copy.start()
    total = mine_ref[...] + recv_ref[rows : rows + 8, :]
    beta_ref[...] = (scale_ref[0:8, :] * total)[:, :HALF]
    eta_ref[...] = (scale_ref[8:16, :] * total)[:, :HALF]
    copies.append(pltpu.make_async_copy(beta_ref, beta_hbm, sems.at[4]))
    copies.append(pltpu.make_async_copy(eta_ref, eta_hbm, sems.at[5]))
    for copy in copies[4:]:
        copy.start()
    for copy in copies:
        copy.wait()


def vmem():
    return pl.BlockSpec(memory_space=pltpu.VMEM)


def smem():
    return pl.BlockSpec(memory_space=pltpu.SMEM)


def hbm():
    return pl.BlockSpec(memory_space=pltpu.HBM)


def held(*dims):
    return vmem(), pltpu.VMEM(dims, F32)


def stored(*dims):
    return hbm(), pltpu.HBM(dims, F32)


def scratch(*dims):
    return pltpu.VMEM(dims, F32)


def run(kernel, name, ins, outs, scratches, args, aliases=None, limit=VMEM_LIMIT):
    return pl.pallas_call(
        kernel,
        in_specs=ins,
        out_specs=[spec for spec, _ in outs],
        out_shape=[shape for _, shape in outs],
        scratch_shapes=scratches,
        input_output_aliases=aliases or {},
        compiler_params=pltpu.CompilerParams(vmem_limit_bytes=limit),
        cost_estimate=pl.CostEstimate(flops=1_000, bytes_accessed=1_000, transcendentals=0),
        name=name,
    )(*args)


def per_device(
    features, rewards, done_flags, traj_len, decay_rate, input_gain, output_gain, value_head
):
    micro_rows, steps_local, width = features.shape
    rows = CHUNK * BLOCKS
    tiles = width // LANES
    swap = [(0, 1), (1, 0)]

    def out(*dims):
        return vmem(), jax.ShapeDtypeStruct(dims, F32)

    def exchange(a, per_block):
        return lax.all_to_all(a, "ctx", 0, 0).reshape(BLOCKS * per_block, LANES)

    (sent,) = run(
        pack_kernel,
        "pack",
        [hbm(), hbm()],
        [out(BLOCKS * (CHUNK + 1), LANES)],
        [
            scratch(steps_local, width),
            pltpu.VMEM((micro_rows, steps_local), jnp.int32),
            pltpu.SemaphoreType.DMA((9,)),
        ],
        (
            pltpu.with_memory_space_constraint(features, pltpu.HBM),
            pltpu.with_memory_space_constraint(done_flags, pltpu.HBM),
        ),
    )
    received = lax.all_to_all(sent.reshape(BLOCKS, CHUNK + 1, 1, LANES), "ctx", 0, 0)
    received = received.reshape(BLOCKS * (CHUNK + 1), LANES)
    own, gain = run(
        rates_kernel,
        "rates",
        [vmem()] * 3,
        [out(2 * K, width), out(2 * K, width)],
        [],
        (-jnp.expm1(-decay_rate[0]), input_gain[0], output_gain[0]),
    )
    other = lax.ppermute(own, "sect", swap)
    head = value_head.reshape(1, width)
    aux, par, scale, power = run(
        tables_kernel,
        "tables",
        [smem()] * 2 + [vmem()] * 5,
        [
            out(AUX_ROWS, LANES),
            out(2, 2 * LANES, LANES),
            out(2 * K, LANES),
            out(2 * HALF, LANES),
        ],
        [],
        (traj_len, done_flags, own, other, gain, head, rewards),
    )
    sent_values, lift0, lift1, slope0, slope1, end0, flags, falls = run(
        forward_kernel,
        "forward",
        [vmem()] * 2,
        [held(BLOCKS * PAYLOAD, LANES)]
        + [held(rows, LANES)] * 4
        + [held(K * 32, LANES)]
        + [held(BLOCKS, LANES)] * 2,
        [scratch(rows, LANES)] * 4 + [scratch(K * 32, LANES)] * 4,
        (received, aux),
    )
    values = exchange(sent_values.reshape(BLOCKS, PAYLOAD, LANES), PAYLOAD)
    sent_carries, small = run(
        backward_kernel,
        "backward",
        [vmem()] * 9,
        [stored(BLOCKS, K, LANES), held(3 * K, LANES)],
        [scratch(rows, LANES)] * 3
        + [scratch(K * 32, LANES)] * 4
        + [scratch(BLOCKS, K, LANES), scratch(BLOCKS, LANES), pltpu.SemaphoreType.DMA((4,))],
        (values, aux, flags, falls, lift0, lift1, slope0, slope1, end0),
    )
    carries = exchange(sent_carries, K)
    others = [lax.ppermute(small, "dp", [(i, i ^ far) for i in range(4)]) for far in (1, 2, 3)]
    by_tile = (
        features.reshape(micro_rows, steps_local // 8, 8, tiles, LANES)
        .transpose(0, 1, 3, 2, 4)
        .reshape(micro_rows, rows, LANES)
    )
    top, local_gs1, local_slope0 = run(
        local_forward_kernel,
        "local_forward",
        [vmem()] * 6,
        [out(rows, LANES)] * 3,
        [scratch(rows, LANES)] * 2 + [scratch(HALF, LANES)],
        (small, by_tile, values, par, power, value_head.reshape(tiles, LANES)),
    )
    keep, send, mine = run(
        local_backward_kernel,
        "local_backward",
        [vmem()] * 10,
        [out(rows, LANES), out(rows + 8, LANES), out(K, LANES)],
        [scratch(rows, LANES)] * 2,
        (carries, par, top, local_gs1, local_slope0, power, small, *others),
    )
    swapped = lax.ppermute(send, "sect", swap)
    (placed,) = run(
        place_kernel,
        "place",
        [vmem()],
        [stored(2, rows, LANES)],
        [pltpu.SemaphoreType.DMA((4,))],
        (keep,),
    )
    grads, grad_beta, grad_eta = run(
        finish_kernel,
        "finish",
        [vmem()] * 3 + [hbm()],
        [stored(2, rows, LANES)] + [stored(K, HALF)] * 2,
        [scratch(K, HALF)] * 2 + [pltpu.SemaphoreType.DMA((6,))],
        (swapped, mine, scale, placed),
        {3: 0},
    )
    grad_inputs = (
        grads.reshape(micro_rows, steps_local // 8, tiles, 8, LANES)
        .transpose(0, 1, 3, 2, 4)
        .reshape(1, micro_rows, steps_local, width)
    )
    return (grad_inputs, grad_beta[None], grad_eta[None])


def solution(mesh):
    placed = (
        P("dp", "ctx", None),
        P("dp", "ctx"),
        P("dp", "ctx"),
        P(),
        P("sect", None, None),
        P("sect", None, None),
        P("sect", None, None),
        P(),
    )
    return jax.shard_map(
        per_device,
        mesh=mesh,
        in_specs=placed,
        out_specs=(P("sect", "dp", "ctx", None), P("sect", None, "ctx"), P("sect", None, "ctx")),
        check_vma=False,
    )
```

```python
import math

import jax
import jax.numpy as jnp
from jax import lax
from jax.experimental import pallas as pl
from jax.experimental.pallas import tpu as pltpu
from jax.sharding import PartitionSpec as P

F32 = jnp.float32
LANES = 128
K = 8
HALF = 64
UNROLL = 8
CHUNK = 32
BLOCKS = 32
VMEM_LIMIT = 12 * 1024 * 1024
AUX_ROWS = 64


def lane_index(shape):
    return lax.broadcasted_iota(jnp.int32, shape, len(shape) - 1)


def lower_lanes(shape):
    return lane_index(shape) < HALF


def swap_halves(a):
    return pltpu.roll(a, HALF, 1)


def gather_lanes(a, lanes):
    return jnp.take_along_axis(a, lanes, axis=1, mode="promise_in_bounds")


def token_lanes():
    return jnp.where(lower_lanes((8, LANES)), 0, CHUNK)


def sigmoid(v):
    return 0.5 * jnp.tanh(0.5 * v) + 0.5


def rows_of(ref, start, stride, size=8):
    return ref[pl.ds(start, size, stride=stride), :]


def pack_kernel(feat_hbm, flag_hbm, out_hbm, feat_ref, flag_ref, out_ref, sems):
    core = lax.axis_index("sect")
    parts = 4
    wide = feat_ref.shape[1] // parts
    tall = out_ref.shape[0] // parts
    flag_copy = pltpu.make_async_copy(flag_hbm, flag_ref, sems.at[2 * parts])
    flag_copy.start()
    arriving, leaving = [], []
    for part in range(parts):
        lanes, rows = pl.ds(part * wide, wide), pl.ds(part * tall, tall)
        arriving.append(
            pltpu.make_async_copy(feat_hbm.at[core, :, lanes], feat_ref.at[:, lanes], sems.at[part])
        )
        leaving.append(
            pltpu.make_async_copy(out_ref.at[rows], out_hbm.at[rows], sems.at[parts + part])
        )
        arriving[-1].start()
    lo = lower_lanes((8, LANES))
    flag_copy.wait()
    flags = flag_ref[pl.ds(core, 1), :].astype(F32)
    row = jnp.concatenate([flags, jnp.zeros((1, HALF), F32)], axis=1)
    for block in range(BLOCKS):
        at = block * (CHUNK + 1) + CHUNK
        out_ref[at : at + 1, :] = row
    for part in range(parts):
        arriving[part].wait()
        for pair in range(part * BLOCKS // (2 * parts), (part + 1) * BLOCKS // (2 * parts)):
            for g in range(CHUNK // 8):
                lanes = slice(pair * LANES, (pair + 1) * LANES)
                early = feat_ref[8 * g : 8 * g + 8, lanes]
                late = feat_ref[CHUNK + 8 * g : CHUNK + 8 * g + 8, lanes]
                even_row = 2 * pair * (CHUNK + 1) + 8 * g
                odd_row = (2 * pair + 1) * (CHUNK + 1) + 8 * g
                out_ref[even_row : even_row + 8, :] = jnp.where(lo, early, swap_halves(late))
                out_ref[odd_row : odd_row + 8, :] = jnp.where(lo, swap_halves(early), late)
        leaving[part].start()
    for copy in leaving:
        copy.wait()


def rates_kernel(p_ref, beta_ref, eta_ref, own_ref, gain_ref):
    p = p_ref[...]
    scale = jnp.sqrt(p * (2.0 - p))
    in_scale = scale * beta_ref[...]
    own_ref[0:8, :] = 1.0 - p
    own_ref[8:16, :] = in_scale * eta_ref[...]
    gain_ref[0:8, :] = scale * eta_ref[...]
    gain_ref[8:16, :] = in_scale


def channel_tile(ref, place, lo_row, rows):
    start = pl.multiple_of((place // 2) * LANES, LANES)
    tile = ref[lo_row : lo_row + rows, pl.ds(start, LANES)]
    flipped = swap_halves(tile)
    lo = lower_lanes((rows, LANES))
    odd = (place % 2) == 1
    return jnp.where(odd, jnp.where(lo, flipped, tile), jnp.where(lo, tile, flipped))


def tables_kernel(
    lens_ref,
    flag_ref,
    own_ref,
    other_ref,
    gain_ref,
    head_ref,
    rewards_ref,
    aux_ref,
    par_ref,
    scale_ref,
    power_ref,
):
    core, place, dp = lax.axis_index("sect"), lax.axis_index("ctx"), lax.axis_index("dp")
    for section in range(2):
        here = core == section
        q = jnp.where(here, channel_tile(own_ref, place, 0, 8), channel_tile(other_ref, place, 0, 8))
        w = jnp.where(here, channel_tile(own_ref, place, 8, 8), channel_tile(other_ref, place, 8, 8))
        aux_ref[16 * section : 16 * section + 8, :] = q
        aux_ref[16 * section + 8 : 16 * section + 16, :] = w
        aux_ref[32 + 8 * section : 40 + 8 * section, :] = power32(q)
        for which in range(2):
            for tile in range(16):
                rows, lanes = slice(8 * which, 8 * which + 8), slice(tile * LANES, (tile + 1) * LANES)
                at = which * LANES + tile * 8
                par_ref[section, at : at + 8, :] = jnp.where(here, own_ref[rows, lanes], other_ref[rows, lanes])
    aux_ref[48:56, :] = jnp.broadcast_to(channel_tile(head_ref, place, 0, 1), (8, LANES))
    rewards = rewards_ref[pl.ds(core, 1), :]
    aux_ref[56:57, :] = jnp.concatenate([rewards, jnp.zeros((1, HALF), F32)], axis=1)
    aux_ref[57:64, :] = jnp.full((7, LANES), lens_ref[dp * 2 + core].astype(F32))
    scale_ref[...] = channel_tile(gain_ref, place, 0, 16)
    rise = jnp.float32(1.0)
    fall = jnp.float32(1.0)
    for t in range(HALF):
        flag = flag_ref[core, t].astype(F32)
        rise = rise * (1.0 + flag)
        fall = fall * (1.0 - 0.5 * flag)
        power_ref[t : t + 1, :] = jnp.full((1, LANES), rise)
        power_ref[HALF + t : HALF + t + 1, :] = jnp.full((1, LANES), fall)


def power32(q):
    for _ in range(5):
        q = q * q
    return q


def spread(a, k):
    return jnp.broadcast_to(a[k : k + 1, :], (8, LANES))


def ends_pass(lifted_ref, q, store_end):
    qs = [spread(q, k) for k in range(K)]
    for pair in range(2):
        groups = (2 * pair, 2 * pair + 1)

        def step(it, state):
            state = list(state)
            for u in range(UNROLL):
                r = it * UNROLL + u
                for i, g in enumerate(groups):
                    lifted = lifted_ref[pl.ds(pl.multiple_of(r * 32 + 8 * g, 8), 8), :]
                    for k in range(K):
                        state[i * K + k] = state[i * K + k] * qs[k] + lifted
            return tuple(state)

        state = lax.fori_loop(0, CHUNK // UNROLL, step, tuple(jnp.zeros((8, LANES), F32) for _ in range(16)))
        for i, g in enumerate(groups):
            for k in range(K):
                store_end(k, g, state[i * K + k])


def halves_of(a):
    flipped = swap_halves(a)
    lo = lower_lanes(a.shape)
    return jnp.where(lo, a, flipped), jnp.where(lo, flipped, a)


def forward_carries(end_ref, fall_ref, q32, carry_ref, in_ref):
    lo = lower_lanes((8, LANES))
    q64 = q32 * q32
    carry = jnp.zeros((8, LANES), F32)
    for block in range(BLOCKS):
        end_early, end_late = halves_of(rows_of(end_ref, block, 32))
        fall_early, fall_late = halves_of(fall_ref[block : block + 1, :])
        entering_late = q32 * fall_early * carry + end_early
        carry_ref[block * 8 : block * 8 + 8, :] = carry
        in_ref[pl.ds(block, 8, stride=32), :] = jnp.where(lo, carry, entering_late)
        block_end = q32 * fall_late * end_early + end_late
        carry = q64 * (fall_early * fall_late) * carry + block_end


def forward_pass(lifted_ref, fall_ref, in_ref, q, w, ema_ref):
    qs = [spread(q, k) for k in range(K)]
    ws = [spread(w, k) for k in range(K)]
    for pair in range(2):
        groups = (2 * pair, 2 * pair + 1)

        def step(it, state):
            state = list(state)
            for u in range(UNROLL):
                r = it * UNROLL + u
                for i, g in enumerate(groups):
                    at = pl.ds(pl.multiple_of(r * 32 + 8 * g, 8), 8)
                    lifted = lifted_ref[at, :]
                    total = None
                    for k in range(K):
                        new = state[i * K + k] * qs[k] + lifted
                        state[i * K + k] = new
                        term = new * ws[k]
                        total = term if total is None else total + term
                    ema_ref[at, :] = total * fall_ref[at, :]
            return tuple(state)

        start = tuple(in_ref[k * 32 + 8 * g : k * 32 + 8 * g + 8, :] for g in groups for k in range(K))
        lax.fori_loop(0, CHUNK // UNROLL, step, start)


def lane_sums(vectors):
    lane = lane_index((8, LANES))
    for bit in range(5):
        mask = (lane & (1 << bit)) == 0
        pairs = [(vectors[2 * m], vectors[2 * m + 1]) for m in range(len(vectors) // 2)]
        vectors = [
            jnp.where(mask, a, b) + gather_lanes(jnp.where(mask, b, a), lane ^ (1 << bit))
            for a, b in pairs
        ]
    v = vectors[0]
    v = v + gather_lanes(v, lane ^ 32)
    return jnp.where(lane < CHUNK, v, pltpu.roll(v, LANES - CHUNK, 1))


PAYLOAD = BLOCKS // 2 + K


def forward_kernel(
    recv_ref,
    aux_ref,
    out_ref,
    lift0_ref,
    lift1_ref,
    slope0_ref,
    slope1_ref,
    end0_ref,
    flags_ref,
    falls_ref,
    rise_ref,
    fall_ref,
    ema_ref,
    hid_ref,
    end1_ref,
    in_ref,
    carry0_ref,
    carry1_ref,
):
    place = lax.axis_index("ctx")
    stride = CHUNK + 1
    q0, w0, q1, w1 = (aux_ref[8 * i : 8 * i + 8, :] for i in range(4))
    lo = lower_lanes((8, LANES))
    lanes = token_lanes()
    for g in range(4):
        flags = rows_of(recv_ref, 8 * g * stride + CHUNK, stride)
        flags_ref[8 * g : 8 * g + 8, :] = flags
        rise = jnp.ones((8, LANES), F32)
        fall = jnp.ones((8, LANES), F32)
        for r in range(CHUNK):
            flag = gather_lanes(flags, lanes + r)
            rise = rise * (1.0 + flag)
            fall = fall * (1.0 - 0.5 * flag)
            at = slice(r * 32 + 8 * g, r * 32 + 8 * g + 8)
            rise_ref[at, :] = rise
            fall_ref[at, :] = fall
            lift0_ref[at, :] = rows_of(recv_ref, 8 * g * stride + r, stride) * rise
        falls_ref[8 * g : 8 * g + 8, :] = fall

    def store(end_ref):
        def one(k, g, u):
            at = slice(k * 32 + 8 * g, k * 32 + 8 * g + 8)
            end_ref[at, :] = u * falls_ref[8 * g : 8 * g + 8, :]

        return one

    ends_pass(lift0_ref, q0, store(end0_ref))
    forward_carries(end0_ref, falls_ref, aux_ref[32:40, :], carry0_ref, in_ref)
    forward_pass(lift0_ref, fall_ref, in_ref, q0, w0, ema_ref)

    def after0(it, _):
        for u in range(8):
            at = pl.ds(pl.multiple_of(it * 64 + 8 * u, 8), 8)
            ema, fall = ema_ref[at, :], fall_ref[at, :]
            sig = sigmoid(ema)
            hidden = lift0_ref[at, :] * fall + ema * sig
            hid_ref[at, :] = hidden
            lift1_ref[at, :] = hidden * rise_ref[at, :]
            slope0_ref[at, :] = sig * (1.0 + ema * (1.0 - sig)) * fall
        return 0

    lax.fori_loop(0, 16, after0, 0)
    ends_pass(lift1_ref, q1, store(end1_ref))
    forward_carries(end1_ref, falls_ref, aux_ref[40:48, :], carry1_ref, in_ref)
    forward_pass(lift1_ref, fall_ref, in_ref, q1, w1, ema_ref)
    head8 = aux_ref[48:56, :]

    def after1(it, _):
        for u in range(8):
            at = pl.ds(pl.multiple_of(it * 64 + 8 * u, 8), 8)
            ema = ema_ref[at, :]
            sig = sigmoid(ema)
            slope1_ref[at, :] = sig * (1.0 + ema * (1.0 - sig)) * fall_ref[at, :]
            hid_ref[at, :] = (hid_ref[at, :] + ema * sig) * head8
        return 0

    lax.fori_loop(0, 16, after1, 0)
    values = jnp.concatenate(
        [
            lane_sums([hid_ref[r * 32 + 8 * g : r * 32 + 8 * g + 8, :] for r in range(CHUNK)])
            for g in range(4)
        ],
        axis=0,
    )
    total = BLOCKS * HALF
    gamma = math.exp(-0.25 / total)
    shape = (BLOCKS, LANES)
    lane = lane_index(shape)
    row = lax.broadcasted_iota(jnp.int32, shape, 0)
    after = (row * HALF + lane + 1).astype(F32)
    next_block = pltpu.roll(pltpu.roll(values, BLOCKS - 1, 0), HALF - 1, 1)
    following = jnp.where(lane == HALF - 1, next_block, pltpu.roll(values, LANES - 1, 1))
    following = jnp.where(after < aux_ref[57:58, :], following, 0.0)
    part = gamma * (1.0 - flags_ref[...]) * following - values
    part = part + jnp.where(row == place, aux_ref[56:57, :], 0.0)
    half_rows = BLOCKS // 2
    packed = jnp.where(
        lower_lanes((half_rows, LANES)), part[:half_rows, :], swap_halves(part[half_rows:, :])
    )
    for block in range(BLOCKS):
        at = block * PAYLOAD
        rows = slice(block * 8, block * 8 + 8)
        out_ref[at : at + half_rows, :] = packed
        out_ref[at + half_rows : at + PAYLOAD, :] = jnp.where(lo, carry0_ref[rows, :], carry1_ref[rows, :])


def starts_pass(grad_ref, q, start_ref, lift_ref=None):
    qs = [spread(q, k) for k in range(K)]
    sums = [jnp.zeros((8, LANES), F32) for _ in range(K)]
    for pair in range(2):
        groups = (2 * pair, 2 * pair + 1)

        def step(it, state):
            state = list(state)
            for u in range(UNROLL):
                r = CHUNK - 1 - (it * UNROLL + u)
                for i, g in enumerate(groups):
                    at = pl.ds(pl.multiple_of(r * 32 + 8 * g, 8), 8)
                    grad = grad_ref[at, :]
                    lifted = None if lift_ref is None else lift_ref[at, :]
                    for k in range(K):
                        new = state[i * K + k] * qs[k] + grad
                        state[i * K + k] = new
                        if lift_ref is not None:
                            state[16 + k] = state[16 + k] + new * lifted
            return tuple(state)

        begin = [jnp.zeros((8, LANES), F32) for _ in range(16)]
        if lift_ref is not None:
            begin = begin + sums
        state = lax.fori_loop(0, CHUNK // UNROLL, step, tuple(begin))
        sums = list(state[16:])
        for i, g in enumerate(groups):
            for k in range(K):
                start_ref[k * 32 + 8 * g : k * 32 + 8 * g + 8, :] = state[i * K + k]
    return sums


def backward_carries(start_ref, fall_ref, q32, carry_ref, in_ref=None, end_ref=None):
    lo = lower_lanes((8, LANES))
    q64 = q32 * q32
    carry = jnp.zeros((8, LANES), F32)
    added = jnp.zeros((8, LANES), F32)
    for block in range(BLOCKS - 1, -1, -1):
        start_early, start_late = halves_of(rows_of(start_ref, block, 32))
        fall_early, fall_late = halves_of(fall_ref[block : block + 1, :])
        entering_early = q32 * fall_late * carry + start_late
        carry_ref[block * 8 : block * 8 + 8, :] = carry
        entering = jnp.where(lo, entering_early, carry)
        if in_ref is not None:
            in_ref[pl.ds(block, 8, stride=32), :] = entering * fall_ref[block : block + 1, :]
        if end_ref is not None:
            added = added + entering * rows_of(end_ref, block, 32)
        block_start = q32 * fall_early * start_late + start_early
        carry = q64 * (fall_early * fall_late) * carry + block_start
    return added


def backward_pass(grad_ref, top_ref, rise_ref, slope_ref, lift_ref, in_ref, q, w, out_ref):
    qs = [spread(q, k) for k in range(K)]
    ws = [spread(w, k) for k in range(K)]
    sums = [jnp.zeros((8, LANES), F32) for _ in range(K)]
    for pair in range(2):
        groups = (2 * pair, 2 * pair + 1)

        def step(it, state):
            state = list(state)
            for u in range(UNROLL):
                r = CHUNK - 1 - (it * UNROLL + u)
                for i, g in enumerate(groups):
                    at = pl.ds(pl.multiple_of(r * 32 + 8 * g, 8), 8)
                    grad = grad_ref[at, :]
                    lifted = lift_ref[at, :]
                    total = None
                    for k in range(K):
                        new = state[i * K + k] * qs[k] + grad
                        state[i * K + k] = new
                        state[16 + k] = state[16 + k] + new * lifted
                        term = new * ws[k]
                        total = term if total is None else total + term
                    out_ref[at, :] = (top_ref[at, :] + rise_ref[at, :] * total) * slope_ref[at, :]
            return tuple(state)

        start = [in_ref[k * 32 + 8 * g : k * 32 + 8 * g + 8, :] for g in groups for k in range(K)]
        state = lax.fori_loop(0, CHUNK // UNROLL, step, tuple(start + sums))
        sums = list(state[16:])
    return sums


def folded(sums):
    return jnp.concatenate([jnp.sum(a, axis=0, keepdims=True) for a in sums], axis=0)


def four_steps(summed, reach, s, axis, index, limit):
    size = summed.shape[axis]

    def later(a, m, beyond):
        return jnp.where(index + m * s < limit, pltpu.roll(a, size - m * s, axis), beyond)

    a1, a2, a3 = (later(summed, m, 0.0) for m in (1, 2, 3))
    r1, r2, r3 = (later(reach, m, 1.0) for m in (1, 2, 3))
    near, far = reach * r1, r2 * r3
    return (summed + reach * a1) + near * (a2 + r2 * a3), near * far


def backward_kernel(
    td_ref,
    aux_ref,
    flags_ref,
    falls_ref,
    lift0_ref,
    lift1_ref,
    slope0_ref,
    slope1_ref,
    end0_ref,
    rise_ref,
    out_hbm,
    small_ref,
    gs_ref,
    top_ref,
    start_ref,
    back0_ref,
    back1_ref,
    in_ref,
    both_ref,
    all_ref,
    sems,
):
    core, place = lax.axis_index("sect"), lax.axis_index("ctx")
    q0, w0, q1, w1 = (aux_ref[8 * i : 8 * i + 8, :] for i in range(4))
    half_rows = BLOCKS // 2
    packed = td_ref[0:half_rows, :]
    for block in range(1, BLOCKS):
        packed = packed + td_ref[block * PAYLOAD : block * PAYLOAD + half_rows, :]
    total = BLOCKS * HALF
    trace = math.exp(-1.0 / total)
    shape = (BLOCKS, LANES)
    lane = lane_index(shape)
    row = lax.broadcasted_iota(jnp.int32, shape, 0)
    valid = ((row * HALF + lane).astype(F32) < aux_ref[57:58, :]) & (lane < HALF)
    td = jnp.where(valid, jnp.concatenate([packed, swap_halves(packed)], axis=0), 0.0)
    reach = trace * (1.0 - flags_ref[...])
    adv = td
    for s in (1, 4, 16):
        adv, reach = four_steps(adv, reach, s, 1, lane, HALF)
    block_adv = jnp.broadcast_to(adv[:, 0:1], shape)
    block_reach = jnp.broadcast_to(reach[:, 0:1], shape)
    for s in (1, 4):
        block_adv, block_reach = four_steps(block_adv, block_reach, s, 0, row, BLOCKS)
    block_adv = block_adv + block_reach * jnp.where(row < 16, pltpu.roll(block_adv, 16, 0), 0.0)
    arriving = jnp.where(row + 1 < BLOCKS, pltpu.roll(block_adv, BLOCKS - 1, 0), 0.0)
    grad = jnp.where(valid, -(adv + reach * arriving), 0.0)
    all_ref[...] = grad
    small_ref[16:24, :] = jnp.broadcast_to(all_ref[pl.ds(place, 1), :], (8, LANES))

    head8 = aux_ref[48:56, :]
    lo = lower_lanes((8, LANES))
    lanes = token_lanes()
    for g in range(4):
        rows = grad[8 * g : 8 * g + 8, :]
        for r in range(CHUNK):
            at = slice(r * 32 + 8 * g, r * 32 + 8 * g + 8)
            top = gather_lanes(rows, lanes + r) * head8
            top_ref[at, :] = top
            gs_ref[at, :] = top * slope1_ref[at, :]

    starts_pass(gs_ref, q1, start_ref)
    backward_carries(start_ref, falls_ref, aux_ref[40:48, :], back1_ref, in_ref)
    sums1 = backward_pass(gs_ref, top_ref, rise_ref, slope0_ref, lift1_ref, in_ref, q1, w1, gs_ref)
    sums0 = starts_pass(gs_ref, q0, start_ref, lift0_ref)
    added0 = backward_carries(start_ref, falls_ref, aux_ref[32:40, :], back0_ref, None, end0_ref)
    copies = []
    for part in range(4):
        for block in range(8 * part, 8 * part + 8):
            at = slice(block * 8, block * 8 + 8)
            both_ref[block] = jnp.where(lo, back1_ref[at, :], back0_ref[at, :])
        piece = pl.ds(8 * part, 8)
        copies.append(pltpu.make_async_copy(both_ref.at[piece], out_hbm.at[piece], sems.at[part]))
        copies[-1].start()
    full0 = folded(sums0) + q0 * added0
    full1 = folded(sums1)
    full0 = full0 + swap_halves(full0)
    full1 = full1 + swap_halves(full1)
    first = core == 0
    small_ref[0:8, :] = jnp.where(first, full0, full1)
    small_ref[8:16, :] = jnp.where(first, full1, full0)
    for copy in copies:
        copy.wait()


def carried(carry_ref, k, rows, base, upper):
    lo = lower_lanes((16, LANES))
    even = carry_ref[pl.ds(base + k, 16, stride=2 * rows), :]
    odd = carry_ref[pl.ds(rows + base + k, 16, stride=2 * rows), :]
    if upper:
        return jnp.where(lo, swap_halves(even), odd)
    return jnp.where(lo, even, swap_halves(odd))


def section_rates(par_ref, section, which):
    return [par_ref[section, pl.ds(which * LANES + k, 16, stride=8), :] for k in range(K)]


def local_forward_kernel(
    small_ref,
    feat_ref,
    carry_ref,
    par_ref,
    power_ref,
    head_ref,
    top_ref,
    gs1_ref,
    slope0_ref,
    ema_ref,
    hid_ref,
    grad_ref,
):
    core = lax.axis_index("sect")
    head = head_ref[...]
    row = small_ref[16:17, :]
    for t in range(HALF):
        grad_ref[t : t + 1, :] = jnp.broadcast_to(row[:, t : t + 1], (1, LANES))

    def across(ref, at):
        return jnp.broadcast_to(ref[pl.ds(at, 1), :], (16, LANES))

    def token(tile, row):
        return pl.ds(tile * LANES + row, 16, stride=8)

    def local(tile, row):
        return pl.ds(pl.multiple_of(tile * LANES + row * 16, 16), 16)

    def forward(section, read):
        qs, ws = section_rates(par_ref, section, 0), section_rates(par_ref, section, 1)

        def step(tile, state):
            state = list(state)
            for row in range(8):
                lifted = read(tile, row) * across(power_ref, tile * 8 + row)
                total = None
                for k in range(K):
                    state[k] = state[k] * qs[k] + lifted
                    term = state[k] * ws[k]
                    total = term if total is None else total + term
                ema_ref[local(tile, row), :] = total * across(power_ref, HALF + tile * 8 + row)
            return tuple(state)

        begin = tuple(carried(carry_ref, k, PAYLOAD, BLOCKS // 2, section == 1) for k in range(K))
        lax.fori_loop(0, HALF // 8, step, begin)

    forward(0, lambda *at: feat_ref[core, token(*at), :])

    def after0(tile, _):
        for row in range(8):
            at = local(tile, row)
            ema = ema_ref[at, :]
            sig = sigmoid(ema)
            hid_ref[at, :] = feat_ref[core, token(tile, row), :] + ema * sig
            fall = across(power_ref, HALF + tile * 8 + row)
            slope0_ref[at, :] = sig * (1.0 + ema * (1.0 - sig)) * fall
        return 0

    lax.fori_loop(0, HALF // 8, after0, 0)
    forward(1, lambda *at: hid_ref[local(*at), :])

    def after1(tile, _):
        for row in range(8):
            at = local(tile, row)
            ema = ema_ref[at, :]
            sig = sigmoid(ema)
            top = head * across(grad_ref, tile * 8 + row)
            top_ref[at, :] = top
            fall = across(power_ref, HALF + tile * 8 + row)
            gs1_ref[at, :] = top * (sig * (1.0 + ema * (1.0 - sig)) * fall)
        return 0

    lax.fori_loop(0, HALF // 8, after1, 0)


def local_backward(half, carry_ref, par_ref, top_ref, gs1_ref, slope0_ref, power_ref, upper_ref, lower_ref, gs0_ref, hid_ref):
    lo = lower_lanes((8, LANES))
    fall_end = jnp.broadcast_to(power_ref[2 * HALF - 1 : 2 * HALF, :], (8, LANES))

    def wide(tile, row):
        return pl.ds(pl.multiple_of(tile * LANES + 16 * row + 8 * half, 8), 8)

    def narrow(tile, row):
        return pl.ds(pl.multiple_of(tile * HALF + 8 * row, 8), 8)

    def out_rows(tile, row):
        return pl.ds(tile * HALF + row, 8, stride=8)

    def entering(k, upper):
        even = carry_ref[pl.ds(8 * half * 16 + k, 8, stride=16), :]
        odd = carry_ref[pl.ds(8 * half * 16 + 8 + k, 8, stride=16), :]
        if upper:
            return jnp.where(lo, swap_halves(even), odd)
        return jnp.where(lo, even, swap_halves(odd))

    def rates(section, which):
        start = which * LANES + half * HALF
        return [par_ref[section, pl.ds(start + k, 8, stride=8), :] for k in range(K)]

    def backward(section, lifted_at, finish):
        qs, ws = rates(section, 0), rates(section, 1)

        def step(it, state):
            state = list(state)
            tile = HALF // 8 - 1 - it
            for row in range(7, -1, -1):
                lifted = lifted_at(tile, row)
                total = None
                for k in range(K):
                    state[k] = state[k] * qs[k] + lifted
                    term = state[k] * ws[k]
                    total = term if total is None else total + term
                rise = jnp.broadcast_to(power_ref[pl.ds(tile * 8 + row, 1), :], (8, LANES))
                finish((tile, row), total * rise)
            return tuple(state)

        begin = tuple(entering(k, section == 0) * fall_end for k in range(K))
        lax.fori_loop(0, HALF // 8, step, begin)

    def finish1(at, added):
        grad = top_ref[wide(*at), :] + added
        upper_ref[out_rows(*at), :] = grad
        hid_ref[narrow(*at), :] = grad
        gs0_ref[narrow(*at), :] = grad * slope0_ref[wide(*at), :]

    def finish0(at, added):
        lower_ref[out_rows(*at), :] = hid_ref[narrow(*at), :] + added

    backward(1, lambda *at: gs1_ref[wide(*at), :], finish1)
    backward(0, lambda *at: gs0_ref[narrow(*at), :], finish0)


def by_core(half, ins, keep_ref, send_ref, scratches):
    core = lax.axis_index("sect")

    @pl.when(core == 0)
    def _():
        local_backward(half, *ins, send_ref, keep_ref, *scratches)

    @pl.when(core == 1)
    def _():
        local_backward(half, *ins, keep_ref, send_ref, *scratches)


def first_half_kernel(*refs):
    ins, (own_ref, *others), (keep_ref, send_ref, mine_ref), scratches = refs[:6], refs[6:10], refs[10:13], refs[13:]
    own, xor1, xor2, xor3 = (ref[0:16, :] for ref in (own_ref, *others))
    total = (own + xor1) + (xor2 + xor3)
    mine_ref[...] = total[0:8, :]
    rows = keep_ref.shape[0]
    send_ref[rows : rows + 8, :] = total[8:16, :]
    by_core(0, ins, keep_ref, send_ref, scratches)


def second_half_kernel(*refs):
    by_core(1, refs[:6], refs[6], refs[7], refs[8:])


def half_copies(ref, out_hbm, slot, half, sems, first):
    return [
        pltpu.make_async_copy(
            ref.at[pl.ds(i * HALF, HALF)], out_hbm.at[slot, i, pl.ds(half * HALF, HALF)], sems.at[first + i]
        )
        for i in range(8)
    ]


def place_kernel(
    keep0_ref,
    keep1_ref,
    recv_ref,
    mine_ref,
    scale_ref,
    out_hbm,
    beta_hbm,
    eta_hbm,
    beta_ref,
    eta_ref,
    sems,
):
    core = lax.axis_index("sect")
    copies = half_copies(keep0_ref, out_hbm, core, 0, sems, 0)
    copies += half_copies(keep1_ref, out_hbm, core, 1, sems, 8)
    copies += half_copies(recv_ref, out_hbm, 1 - core, 0, sems, 16)
    for copy in copies:
        copy.start()
    rows = keep0_ref.shape[0]
    total = mine_ref[...] + recv_ref[rows : rows + 8, :]
    beta_ref[...] = (scale_ref[0:8, :] * total)[:, :HALF]
    eta_ref[...] = (scale_ref[8:16, :] * total)[:, :HALF]
    small = [
        pltpu.make_async_copy(beta_ref, beta_hbm, sems.at[24]),
        pltpu.make_async_copy(eta_ref, eta_hbm, sems.at[25]),
    ]
    for copy in small:
        copy.start()
    for copy in copies + small:
        copy.wait()


def finish_kernel(recv_ref, placed_hbm, out_hbm, sems):
    del placed_hbm
    copies = half_copies(recv_ref, out_hbm, 1 - lax.axis_index("sect"), 1, sems, 0)
    for copy in copies:
        copy.start()
    for copy in copies:
        copy.wait()


def vmem():
    return pl.BlockSpec(memory_space=pltpu.VMEM)


def smem():
    return pl.BlockSpec(memory_space=pltpu.SMEM)


def hbm():
    return pl.BlockSpec(memory_space=pltpu.HBM)


def held(*dims):
    return vmem(), pltpu.VMEM(dims, F32)


def stored(*dims):
    return hbm(), pltpu.HBM(dims, F32)


def scratch(*dims):
    return pltpu.VMEM(dims, F32)


def run(kernel, name, ins, outs, scratches, args, aliases=None, limit=VMEM_LIMIT):
    return pl.pallas_call(
        kernel,
        in_specs=ins,
        out_specs=[spec for spec, _ in outs],
        out_shape=[shape for _, shape in outs],
        scratch_shapes=scratches,
        input_output_aliases=aliases or {},
        compiler_params=pltpu.CompilerParams(vmem_limit_bytes=limit),
        cost_estimate=pl.CostEstimate(flops=1_000, bytes_accessed=1_000, transcendentals=0),
        name=name,
    )(*args)


def per_device(
    features, rewards, done_flags, traj_len, decay_rate, input_gain, output_gain, value_head
):
    micro_rows, steps_local, width = features.shape
    rows = CHUNK * BLOCKS
    tiles = width // LANES
    swap = [(0, 1), (1, 0)]

    def out(*dims):
        return vmem(), jax.ShapeDtypeStruct(dims, F32)

    def exchange(a, per_block):
        return lax.all_to_all(a, "ctx", 0, 0).reshape(BLOCKS * per_block, LANES)

    (sent,) = run(
        pack_kernel,
        "pack",
        [hbm(), hbm()],
        [stored(BLOCKS * (CHUNK + 1), LANES)],
        [
            scratch(steps_local, width),
            pltpu.VMEM((micro_rows, steps_local), jnp.int32),
            scratch(BLOCKS * (CHUNK + 1), LANES),
            pltpu.SemaphoreType.DMA((9,)),
        ],
        (
            pltpu.with_memory_space_constraint(features, pltpu.HBM),
            pltpu.with_memory_space_constraint(done_flags, pltpu.HBM),
        ),
    )
    received = lax.all_to_all(sent.reshape(BLOCKS, CHUNK + 1, 1, LANES), "ctx", 0, 0)
    received = received.reshape(BLOCKS * (CHUNK + 1), LANES)
    own, gain = run(
        rates_kernel,
        "rates",
        [vmem()] * 3,
        [out(2 * K, width), out(2 * K, width)],
        [],
        (-jnp.expm1(-decay_rate[0]), input_gain[0], output_gain[0]),
    )
    other = lax.ppermute(own, "sect", swap)
    head = value_head.reshape(1, width)
    aux, par, scale, power = run(
        tables_kernel,
        "tables",
        [smem()] * 2 + [vmem()] * 5,
        [
            out(AUX_ROWS, LANES),
            out(2, 2 * LANES, LANES),
            out(2 * K, LANES),
            out(2 * HALF, LANES),
        ],
        [],
        (traj_len, done_flags, own, other, gain, head, rewards),
    )
    sent_values, lift0, lift1, slope0, slope1, end0, flags, falls, rise = run(
        forward_kernel,
        "forward",
        [vmem()] * 2,
        [held(BLOCKS * PAYLOAD, LANES)]
        + [held(rows, LANES)] * 4
        + [held(K * 32, LANES)]
        + [held(BLOCKS, LANES)] * 2
        + [held(rows, LANES)],
        [scratch(rows, LANES)] * 3 + [scratch(K * 32, LANES)] * 4,
        (received, aux),
    )
    values = exchange(sent_values.reshape(BLOCKS, PAYLOAD, LANES), PAYLOAD)
    sent_carries, small = run(
        backward_kernel,
        "backward",
        [vmem()] * 10,
        [stored(BLOCKS, K, LANES), held(3 * K, LANES)],
        [scratch(rows, LANES)] * 2
        + [scratch(K * 32, LANES)] * 4
        + [scratch(BLOCKS, K, LANES), scratch(BLOCKS, LANES), pltpu.SemaphoreType.DMA((4,))],
        (values, aux, flags, falls, lift0, lift1, slope0, slope1, end0, rise),
    )
    carries = exchange(sent_carries, K)
    others = [lax.ppermute(small, "dp", [(i, i ^ far) for i in range(4)]) for far in (1, 2, 3)]
    by_tile = (
        features.reshape(micro_rows, steps_local // 8, 8, tiles, LANES)
        .transpose(0, 1, 3, 2, 4)
        .reshape(micro_rows, rows, LANES)
    )
    top, local_gs1, local_slope0 = run(
        local_forward_kernel,
        "local_forward",
        [vmem()] * 6,
        [out(rows, LANES)] * 3,
        [scratch(rows, LANES)] * 2 + [scratch(HALF, LANES)],
        (small, by_tile, values, par, power, value_head.reshape(tiles, LANES)),
    )
    local = (carries, par, top, local_gs1, local_slope0, power)
    half_rows = rows // 2
    keep0, send0, mine = run(
        first_half_kernel,
        "local_backward0",
        [vmem()] * 10,
        [out(half_rows, LANES), out(half_rows + 8, LANES), out(K, LANES)],
        [scratch(half_rows, LANES)] * 2,
        (*local, small, *others),
    )
    swapped0 = lax.ppermute(send0, "sect", swap)
    keep1, send1 = run(
        second_half_kernel,
        "local_backward1",
        [vmem()] * 6,
        [out(half_rows, LANES), out(half_rows, LANES)],
        [scratch(half_rows, LANES)] * 2,
        local,
    )
    swapped1 = lax.ppermute(send1, "sect", swap)
    placed, grad_beta, grad_eta = run(
        place_kernel,
        "place",
        [vmem()] * 5,
        [stored(2, 8, LANES, LANES), stored(K, HALF), stored(K, HALF)],
        [scratch(K, HALF)] * 2 + [pltpu.SemaphoreType.DMA((26,))],
        (keep0, keep1, swapped0, mine, scale),
    )
    (grads,) = run(
        finish_kernel,
        "finish",
        [vmem(), hbm()],
        [stored(2, 8, LANES, LANES)],
        [pltpu.SemaphoreType.DMA((8,))],
        (swapped1, placed),
        {1: 0},
    )
    grad_inputs = (
        grads.reshape(micro_rows, steps_local // 8, tiles, 8, LANES)
        .transpose(0, 1, 3, 2, 4)
        .reshape(1, micro_rows, steps_local, width)
    )
    return (grad_inputs, grad_beta[None], grad_eta[None])


def solution(mesh):
    placed = (
        P("dp", "ctx", None),
        P("dp", "ctx"),
        P("dp", "ctx"),
        P(),
        P("sect", None, None),
        P("sect", None, None),
        P("sect", None, None),
        P(),
    )
    return jax.shard_map(
        per_device,
        mesh=mesh,
        in_specs=placed,
        out_specs=(P("sect", "dp", "ctx", None), P("sect", None, "ctx"), P("sect", None, "ctx")),
        check_vma=False,
    )
```

```python
import math

import jax
import jax.numpy as jnp
from jax import lax
from jax.experimental import pallas as pl
from jax.experimental.pallas import tpu as pltpu
from jax.sharding import PartitionSpec as P

F32 = jnp.float32
LANES = 128
K = 8
HALF = 64
UNROLL = 8
CHUNK = 32
BLOCKS = 32
VMEM_LIMIT = 12 * 1024 * 1024
AUX_ROWS = 64


def lane_index(shape):
    return lax.broadcasted_iota(jnp.int32, shape, len(shape) - 1)


def lower_lanes(shape):
    return lane_index(shape) < HALF


def swap_halves(a):
    return pltpu.roll(a, HALF, 1)


def gather_lanes(a, lanes):
    return jnp.take_along_axis(a, lanes, axis=1, mode="promise_in_bounds")


def token_lanes():
    return jnp.where(lower_lanes((8, LANES)), 0, CHUNK)


def sigmoid(v):
    return 0.5 * jnp.tanh(0.5 * v) + 0.5


def rows_of(ref, start, stride, size=8):
    return ref[pl.ds(start, size, stride=stride), :]


def pack_kernel(feat_hbm, flag_hbm, out_hbm, feat_ref, flag_ref, out_ref, sems):
    core = lax.axis_index("sect")
    parts = 4
    wide = feat_ref.shape[1] // parts
    tall = out_ref.shape[0] // parts
    flag_copy = pltpu.make_async_copy(flag_hbm, flag_ref, sems.at[2 * parts])
    flag_copy.start()
    arriving, leaving = [], []
    for part in range(parts):
        lanes, rows = pl.ds(part * wide, wide), pl.ds(part * tall, tall)
        arriving.append(
            pltpu.make_async_copy(feat_hbm.at[core, :, lanes], feat_ref.at[:, lanes], sems.at[part])
        )
        leaving.append(
            pltpu.make_async_copy(out_ref.at[rows], out_hbm.at[rows], sems.at[parts + part])
        )
        arriving[-1].start()
    lo = lower_lanes((8, LANES))
    flag_copy.wait()
    flags = flag_ref[pl.ds(core, 1), :].astype(F32)
    row = jnp.concatenate([flags, jnp.zeros((1, HALF), F32)], axis=1)
    for block in range(BLOCKS):
        at = block * (CHUNK + 1) + CHUNK
        out_ref[at : at + 1, :] = row
    for part in range(parts):
        arriving[part].wait()
        for pair in range(part * BLOCKS // (2 * parts), (part + 1) * BLOCKS // (2 * parts)):
            for g in range(CHUNK // 8):
                lanes = slice(pair * LANES, (pair + 1) * LANES)
                early = feat_ref[8 * g : 8 * g + 8, lanes]
                late = feat_ref[CHUNK + 8 * g : CHUNK + 8 * g + 8, lanes]
                even_row = 2 * pair * (CHUNK + 1) + 8 * g
                odd_row = (2 * pair + 1) * (CHUNK + 1) + 8 * g
                out_ref[even_row : even_row + 8, :] = jnp.where(lo, early, swap_halves(late))
                out_ref[odd_row : odd_row + 8, :] = jnp.where(lo, swap_halves(early), late)
        leaving[part].start()
    for copy in leaving:
        copy.wait()


def rates_kernel(p_ref, beta_ref, eta_ref, own_ref, gain_ref):
    p = p_ref[...]
    scale = jnp.sqrt(p * (2.0 - p))
    in_scale = scale * beta_ref[...]
    own_ref[0:8, :] = 1.0 - p
    own_ref[8:16, :] = in_scale * eta_ref[...]
    gain_ref[0:8, :] = scale * eta_ref[...]
    gain_ref[8:16, :] = in_scale


def channel_tile(ref, place, lo_row, rows):
    start = pl.multiple_of((place // 2) * LANES, LANES)
    tile = ref[lo_row : lo_row + rows, pl.ds(start, LANES)]
    flipped = swap_halves(tile)
    lo = lower_lanes((rows, LANES))
    odd = (place % 2) == 1
    return jnp.where(odd, jnp.where(lo, flipped, tile), jnp.where(lo, tile, flipped))


def tables_kernel(
    lens_ref,
    flag_ref,
    own_ref,
    other_ref,
    gain_ref,
    head_ref,
    rewards_ref,
    aux_ref,
    par_ref,
    scale_ref,
    power_ref,
):
    core, place, dp = lax.axis_index("sect"), lax.axis_index("ctx"), lax.axis_index("dp")
    for section in range(2):
        here = core == section
        q = jnp.where(here, channel_tile(own_ref, place, 0, 8), channel_tile(other_ref, place, 0, 8))
        w = jnp.where(here, channel_tile(own_ref, place, 8, 8), channel_tile(other_ref, place, 8, 8))
        aux_ref[16 * section : 16 * section + 8, :] = q
        aux_ref[16 * section + 8 : 16 * section + 16, :] = w
        aux_ref[32 + 8 * section : 40 + 8 * section, :] = power32(q)
        for which in range(2):
            for tile in range(16):
                rows, lanes = slice(8 * which, 8 * which + 8), slice(tile * LANES, (tile + 1) * LANES)
                at = which * LANES + tile * 8
                par_ref[section, at : at + 8, :] = jnp.where(here, own_ref[rows, lanes], other_ref[rows, lanes])
    aux_ref[48:56, :] = jnp.broadcast_to(channel_tile(head_ref, place, 0, 1), (8, LANES))
    rewards = rewards_ref[pl.ds(core, 1), :]
    aux_ref[56:57, :] = jnp.concatenate([rewards, jnp.zeros((1, HALF), F32)], axis=1)
    aux_ref[57:64, :] = jnp.full((7, LANES), lens_ref[dp * 2 + core].astype(F32))
    scale_ref[...] = channel_tile(gain_ref, place, 0, 16)
    rise = jnp.float32(1.0)
    fall = jnp.float32(1.0)
    for t in range(HALF):
        flag = flag_ref[core, t].astype(F32)
        rise = rise * (1.0 + flag)
        fall = fall * (1.0 - 0.5 * flag)
        power_ref[t : t + 1, :] = jnp.full((1, LANES), rise)
        power_ref[HALF + t : HALF + t + 1, :] = jnp.full((1, LANES), fall)


def power32(q):
    for _ in range(5):
        q = q * q
    return q


def spread(a, k):
    return jnp.broadcast_to(a[k : k + 1, :], (8, LANES))


def ends_pass(lifted_ref, q, store_end):
    qs = [spread(q, k) for k in range(K)]
    for pair in range(2):
        groups = (2 * pair, 2 * pair + 1)

        def step(it, state):
            state = list(state)
            for u in range(UNROLL):
                r = it * UNROLL + u
                for i, g in enumerate(groups):
                    lifted = lifted_ref[pl.ds(pl.multiple_of(r * 32 + 8 * g, 8), 8), :]
                    for k in range(K):
                        state[i * K + k] = state[i * K + k] * qs[k] + lifted
            return tuple(state)

        state = lax.fori_loop(0, CHUNK // UNROLL, step, tuple(jnp.zeros((8, LANES), F32) for _ in range(16)))
        for i, g in enumerate(groups):
            for k in range(K):
                store_end(k, g, state[i * K + k])


def at_row(r, g):
    return pl.ds(pl.multiple_of(r * 32 + 8 * g, 8), 8)


def halves_of(a):
    flipped = swap_halves(a)
    lo = lower_lanes(a.shape)
    return jnp.where(lo, a, flipped), jnp.where(lo, flipped, a)


def forward_carries(end_ref, fall_ref, q32, carry_ref, in_ref):
    lo = lower_lanes((8, LANES))
    q64 = q32 * q32
    carry = jnp.zeros((8, LANES), F32)
    for block in range(BLOCKS):
        end_early, end_late = halves_of(rows_of(end_ref, block, 32))
        fall_early, fall_late = halves_of(fall_ref[block : block + 1, :])
        entering_late = q32 * fall_early * carry + end_early
        carry_ref[block * 8 : block * 8 + 8, :] = carry
        in_ref[pl.ds(block, 8, stride=32), :] = jnp.where(lo, carry, entering_late)
        block_end = q32 * fall_late * end_early + end_late
        carry = q64 * (fall_early * fall_late) * carry + block_end


def forward_pass(lifted_ref, fall_ref, in_ref, q, w, ema_ref):
    qs = [spread(q, k) for k in range(K)]
    ws = [spread(w, k) for k in range(K)]
    for pair in range(2):
        groups = (2 * pair, 2 * pair + 1)

        def step(it, state):
            state = list(state)
            for u in range(UNROLL):
                r = it * UNROLL + u
                for i, g in enumerate(groups):
                    at = pl.ds(pl.multiple_of(r * 32 + 8 * g, 8), 8)
                    lifted = lifted_ref[at, :]
                    total = None
                    for k in range(K):
                        new = state[i * K + k] * qs[k] + lifted
                        state[i * K + k] = new
                        term = new * ws[k]
                        total = term if total is None else total + term
                    ema_ref[at, :] = total * fall_ref[at, :]
            return tuple(state)

        start = tuple(in_ref[k * 32 + 8 * g : k * 32 + 8 * g + 8, :] for g in groups for k in range(K))
        lax.fori_loop(0, CHUNK // UNROLL, step, start)


def lane_sums(vectors, bits):
    lane = lane_index((8, LANES))
    for bit in bits:
        mask = (lane & (1 << bit)) == 0
        pairs = [(vectors[2 * m], vectors[2 * m + 1]) for m in range(len(vectors) // 2)]
        vectors = [
            jnp.where(mask, a, b) + gather_lanes(jnp.where(mask, b, a), lane ^ (1 << bit))
            for a, b in pairs
        ]
    return vectors[0]


def last_lane_sums(vectors):
    lane = lane_index((8, LANES))
    v = lane_sums(vectors, (3, 4))
    v = v + gather_lanes(v, lane ^ 32)
    return jnp.where(lane < CHUNK, v, pltpu.roll(v, LANES - CHUNK, 1))


PAYLOAD = BLOCKS // 2 + K


def forward_kernel(
    recv_ref,
    aux_ref,
    out_ref,
    lift0_ref,
    lift1_ref,
    slope0_ref,
    slope1_ref,
    end0_ref,
    flags_ref,
    falls_ref,
    rise_ref,
    fall_ref,
    ema_ref,
    hid_ref,
    end1_ref,
    in_ref,
    carry0_ref,
    carry1_ref,
):
    place = lax.axis_index("ctx")
    stride = CHUNK + 1
    q0, w0, q1, w1 = (aux_ref[8 * i : 8 * i + 8, :] for i in range(4))
    lo = lower_lanes((8, LANES))
    lanes = token_lanes()

    for g in range(4):
        flags = rows_of(recv_ref, 8 * g * stride + CHUNK, stride)
        flags_ref[8 * g : 8 * g + 8, :] = flags
        rise = jnp.ones((8, LANES), F32)
        fall = jnp.ones((8, LANES), F32)
        for r in range(CHUNK):
            flag = gather_lanes(flags, lanes + r)
            rise = rise * (1.0 + flag)
            fall = fall * (1.0 - 0.5 * flag)
            at = slice(r * 32 + 8 * g, r * 32 + 8 * g + 8)
            rise_ref[at, :] = rise
            fall_ref[at, :] = fall
            lift0_ref[at, :] = rows_of(recv_ref, 8 * g * stride + r, stride) * rise
        falls_ref[8 * g : 8 * g + 8, :] = fall

    def store(end_ref):
        def one(k, g, u):
            at = slice(k * 32 + 8 * g, k * 32 + 8 * g + 8)
            end_ref[at, :] = u * falls_ref[8 * g : 8 * g + 8, :]

        return one

    ends_pass(lift0_ref, q0, store(end0_ref))
    forward_carries(end0_ref, falls_ref, aux_ref[32:40, :], carry0_ref, in_ref)
    forward_pass(lift0_ref, fall_ref, in_ref, q0, w0, ema_ref)

    def after0(it, _):
        for u in range(8):
            at = pl.ds(pl.multiple_of(it * 64 + 8 * u, 8), 8)
            ema, fall = ema_ref[at, :], fall_ref[at, :]
            sig = sigmoid(ema)
            hidden = lift0_ref[at, :] * fall + ema * sig
            hid_ref[at, :] = hidden
            lift1_ref[at, :] = hidden * rise_ref[at, :]
            slope0_ref[at, :] = sig * (1.0 + ema * (1.0 - sig)) * fall
        return 0

    lax.fori_loop(0, 16, after0, 0)
    ends_pass(lift1_ref, q1, store(end1_ref))
    forward_carries(end1_ref, falls_ref, aux_ref[40:48, :], carry1_ref, in_ref)
    forward_pass(lift1_ref, fall_ref, in_ref, q1, w1, ema_ref)
    head8 = aux_ref[48:56, :]

    parts = []
    for g in range(4):
        for first in range(0, CHUNK, 8):
            tops = []
            for r in range(first, first + 8):
                at = slice(r * 32 + 8 * g, r * 32 + 8 * g + 8)
                ema = ema_ref[at, :]
                sig = sigmoid(ema)
                slope1_ref[at, :] = sig * (1.0 + ema * (1.0 - sig)) * fall_ref[at, :]
                tops.append((hid_ref[at, :] + ema * sig) * head8)
            parts.append(lane_sums(tops, (0, 1, 2)))
    values = jnp.concatenate([last_lane_sums(parts[4 * g : 4 * g + 4]) for g in range(4)], axis=0)
    total = BLOCKS * HALF
    gamma = math.exp(-0.25 / total)
    shape = (BLOCKS, LANES)
    lane = lane_index(shape)
    row = lax.broadcasted_iota(jnp.int32, shape, 0)
    after = (row * HALF + lane + 1).astype(F32)
    next_block = pltpu.roll(pltpu.roll(values, BLOCKS - 1, 0), HALF - 1, 1)
    following = jnp.where(lane == HALF - 1, next_block, pltpu.roll(values, LANES - 1, 1))
    following = jnp.where(after < aux_ref[57:58, :], following, 0.0)
    part = gamma * (1.0 - flags_ref[...]) * following - values
    part = part + jnp.where(row == place, aux_ref[56:57, :], 0.0)
    half_rows = BLOCKS // 2
    packed = jnp.where(
        lower_lanes((half_rows, LANES)), part[:half_rows, :], swap_halves(part[half_rows:, :])
    )
    for block in range(BLOCKS):
        at = block * PAYLOAD
        rows = slice(block * 8, block * 8 + 8)
        out_ref[at : at + half_rows, :] = packed
        out_ref[at + half_rows : at + PAYLOAD, :] = jnp.where(lo, carry0_ref[rows, :], carry1_ref[rows, :])


def starts_pass(grad_ref, q, start_ref, lift_ref=None):
    qs = [spread(q, k) for k in range(K)]
    sums = [jnp.zeros((8, LANES), F32) for _ in range(K)]
    for pair in range(2):
        groups = (2 * pair, 2 * pair + 1)

        def step(it, state):
            state = list(state)
            for u in range(UNROLL):
                r = CHUNK - 1 - (it * UNROLL + u)
                for i, g in enumerate(groups):
                    grad = grad_ref[at_row(r, g), :]
                    lifted = None if lift_ref is None else lift_ref[at_row(r, g), :]
                    for k in range(K):
                        new = state[i * K + k] * qs[k] + grad
                        state[i * K + k] = new
                        if lift_ref is not None:
                            state[16 + k] = state[16 + k] + new * lifted
            return tuple(state)

        begin = [jnp.zeros((8, LANES), F32) for _ in range(16)]
        if lift_ref is not None:
            begin = begin + sums
        state = lax.fori_loop(0, CHUNK // UNROLL, step, tuple(begin))
        sums = list(state[16:])
        for i, g in enumerate(groups):
            for k in range(K):
                start_ref[k * 32 + 8 * g : k * 32 + 8 * g + 8, :] = state[i * K + k]
    return sums


def backward_carries(start_ref, fall_ref, q32, carry_ref, in_ref=None, end_ref=None):
    lo = lower_lanes((8, LANES))
    q64 = q32 * q32
    carry = jnp.zeros((8, LANES), F32)
    added = jnp.zeros((8, LANES), F32)
    for block in range(BLOCKS - 1, -1, -1):
        start_early, start_late = halves_of(rows_of(start_ref, block, 32))
        fall_early, fall_late = halves_of(fall_ref[block : block + 1, :])
        entering_early = q32 * fall_late * carry + start_late
        carry_ref[block * 8 : block * 8 + 8, :] = carry
        entering = jnp.where(lo, entering_early, carry)
        if in_ref is not None:
            in_ref[pl.ds(block, 8, stride=32), :] = entering * fall_ref[block : block + 1, :]
        if end_ref is not None:
            added = added + entering * rows_of(end_ref, block, 32)
        block_start = q32 * fall_early * start_late + start_early
        carry = q64 * (fall_early * fall_late) * carry + block_start
    return added


def backward_pass(grad_ref, top_ref, rise_ref, slope_ref, lift_ref, in_ref, q, w, out_ref):
    qs = [spread(q, k) for k in range(K)]
    ws = [spread(w, k) for k in range(K)]
    sums = [jnp.zeros((8, LANES), F32) for _ in range(K)]
    for pair in range(2):
        groups = (2 * pair, 2 * pair + 1)

        def step(it, state):
            state = list(state)
            for u in range(UNROLL):
                r = CHUNK - 1 - (it * UNROLL + u)
                for i, g in enumerate(groups):
                    at = pl.ds(pl.multiple_of(r * 32 + 8 * g, 8), 8)
                    grad = grad_ref[at, :]
                    lifted = lift_ref[at, :]
                    total = None
                    for k in range(K):
                        new = state[i * K + k] * qs[k] + grad
                        state[i * K + k] = new
                        state[16 + k] = state[16 + k] + new * lifted
                        term = new * ws[k]
                        total = term if total is None else total + term
                    out_ref[at, :] = (top_ref[at, :] + rise_ref[at, :] * total) * slope_ref[at, :]
            return tuple(state)

        start = [in_ref[k * 32 + 8 * g : k * 32 + 8 * g + 8, :] for g in groups for k in range(K)]
        state = lax.fori_loop(0, CHUNK // UNROLL, step, tuple(start + sums))
        sums = list(state[16:])
    return sums


def folded(sums):
    return jnp.concatenate([jnp.sum(a, axis=0, keepdims=True) for a in sums], axis=0)


def four_steps(summed, reach, s, axis, index, limit):
    size = summed.shape[axis]

    def later(a, m, beyond):
        return jnp.where(index + m * s < limit, pltpu.roll(a, size - m * s, axis), beyond)

    a1, a2, a3 = (later(summed, m, 0.0) for m in (1, 2, 3))
    r1, r2, r3 = (later(reach, m, 1.0) for m in (1, 2, 3))
    near, far = reach * r1, r2 * r3
    return (summed + reach * a1) + near * (a2 + r2 * a3), near * far


def backward_kernel(
    td_ref,
    aux_ref,
    flags_ref,
    falls_ref,
    lift0_ref,
    lift1_ref,
    slope0_ref,
    slope1_ref,
    end0_ref,
    rise_ref,
    out_hbm,
    small_ref,
    gs_ref,
    top_ref,
    start_ref,
    back0_ref,
    back1_ref,
    in_ref,
    both_ref,
    all_ref,
    sems,
):
    core, place = lax.axis_index("sect"), lax.axis_index("ctx")
    q0, w0, q1, w1 = (aux_ref[8 * i : 8 * i + 8, :] for i in range(4))
    half_rows = BLOCKS // 2
    packed = td_ref[0:half_rows, :]
    for block in range(1, BLOCKS):
        packed = packed + td_ref[block * PAYLOAD : block * PAYLOAD + half_rows, :]
    total = BLOCKS * HALF
    trace = math.exp(-1.0 / total)
    shape = (BLOCKS, LANES)
    lane = lane_index(shape)
    row = lax.broadcasted_iota(jnp.int32, shape, 0)
    valid = ((row * HALF + lane).astype(F32) < aux_ref[57:58, :]) & (lane < HALF)
    td = jnp.where(valid, jnp.concatenate([packed, swap_halves(packed)], axis=0), 0.0)
    reach = trace * (1.0 - flags_ref[...])
    adv = td
    for s in (1, 4, 16):
        adv, reach = four_steps(adv, reach, s, 1, lane, HALF)
    block_adv = jnp.broadcast_to(adv[:, 0:1], shape)
    block_reach = jnp.broadcast_to(reach[:, 0:1], shape)
    for s in (1, 4):
        block_adv, block_reach = four_steps(block_adv, block_reach, s, 0, row, BLOCKS)
    block_adv = block_adv + block_reach * jnp.where(row < 16, pltpu.roll(block_adv, 16, 0), 0.0)
    arriving = jnp.where(row + 1 < BLOCKS, pltpu.roll(block_adv, BLOCKS - 1, 0), 0.0)
    grad = jnp.where(valid, -(adv + reach * arriving), 0.0)
    all_ref[...] = grad
    small_ref[16:24, :] = jnp.broadcast_to(all_ref[pl.ds(place, 1), :], (8, LANES))

    head8 = aux_ref[48:56, :]
    lo = lower_lanes((8, LANES))
    lanes = token_lanes()
    for g in range(4):
        rows = grad[8 * g : 8 * g + 8, :]
        for r in range(CHUNK):
            at = slice(r * 32 + 8 * g, r * 32 + 8 * g + 8)
            top = gather_lanes(rows, lanes + r) * head8
            top_ref[at, :] = top
            gs_ref[at, :] = top * slope1_ref[at, :]

    starts_pass(gs_ref, q1, start_ref)
    backward_carries(start_ref, falls_ref, aux_ref[40:48, :], back1_ref, in_ref)
    sums1 = backward_pass(gs_ref, top_ref, rise_ref, slope0_ref, lift1_ref, in_ref, q1, w1, gs_ref)
    sums0 = starts_pass(gs_ref, q0, start_ref, lift0_ref)
    added0 = backward_carries(start_ref, falls_ref, aux_ref[32:40, :], back0_ref, None, end0_ref)
    copies = []
    for part in range(4):
        for block in range(8 * part, 8 * part + 8):
            at = slice(block * 8, block * 8 + 8)
            both_ref[block] = jnp.where(lo, back1_ref[at, :], back0_ref[at, :])
        piece = pl.ds(8 * part, 8)
        copies.append(pltpu.make_async_copy(both_ref.at[piece], out_hbm.at[piece], sems.at[part]))
        copies[-1].start()
    full0 = folded(sums0) + q0 * added0
    full1 = folded(sums1)
    full0 = full0 + swap_halves(full0)
    full1 = full1 + swap_halves(full1)
    first = core == 0
    small_ref[0:8, :] = jnp.where(first, full0, full1)
    small_ref[8:16, :] = jnp.where(first, full1, full0)
    for copy in copies:
        copy.wait()


def carried(carry_ref, k, rows, base, upper):
    lo = lower_lanes((16, LANES))
    even = carry_ref[pl.ds(base + k, 16, stride=2 * rows), :]
    odd = carry_ref[pl.ds(rows + base + k, 16, stride=2 * rows), :]
    if upper:
        return jnp.where(lo, swap_halves(even), odd)
    return jnp.where(lo, even, swap_halves(odd))


def section_rates(par_ref, section, which):
    return [par_ref[section, pl.ds(which * LANES + k, 16, stride=8), :] for k in range(K)]


def local_forward_kernel(
    small_ref,
    feat_ref,
    carry_ref,
    par_ref,
    power_ref,
    head_ref,
    top_ref,
    gs1_ref,
    slope0_ref,
    ema_ref,
    hid_ref,
    grad_ref,
):
    core = lax.axis_index("sect")
    head = head_ref[...]
    row = small_ref[16:17, :]
    for t in range(HALF):
        grad_ref[t : t + 1, :] = jnp.broadcast_to(row[:, t : t + 1], (1, LANES))

    def across(ref, at):
        return jnp.broadcast_to(ref[pl.ds(at, 1), :], (16, LANES))

    def token(tile, row):
        return pl.ds(tile * LANES + row, 16, stride=8)

    def local(tile, row):
        return pl.ds(pl.multiple_of(tile * LANES + row * 16, 16), 16)

    def forward(section, read):
        qs, ws = section_rates(par_ref, section, 0), section_rates(par_ref, section, 1)

        def step(tile, state):
            state = list(state)
            for row in range(8):
                lifted = read(tile, row) * across(power_ref, tile * 8 + row)
                total = None
                for k in range(K):
                    state[k] = state[k] * qs[k] + lifted
                    term = state[k] * ws[k]
                    total = term if total is None else total + term
                ema_ref[local(tile, row), :] = total * across(power_ref, HALF + tile * 8 + row)
            return tuple(state)

        begin = tuple(carried(carry_ref, k, PAYLOAD, BLOCKS // 2, section == 1) for k in range(K))
        lax.fori_loop(0, HALF // 8, step, begin)

    forward(0, lambda *at: feat_ref[core, token(*at), :])

    def after0(tile, _):
        for row in range(8):
            at = local(tile, row)
            ema = ema_ref[at, :]
            sig = sigmoid(ema)
            hid_ref[at, :] = feat_ref[core, token(tile, row), :] + ema * sig
            fall = across(power_ref, HALF + tile * 8 + row)
            slope0_ref[at, :] = sig * (1.0 + ema * (1.0 - sig)) * fall
        return 0

    lax.fori_loop(0, HALF // 8, after0, 0)
    forward(1, lambda *at: hid_ref[local(*at), :])

    def after1(tile, _):
        for row in range(8):
            at = local(tile, row)
            ema = ema_ref[at, :]
            sig = sigmoid(ema)
            top = head * across(grad_ref, tile * 8 + row)
            top_ref[at, :] = top
            fall = across(power_ref, HALF + tile * 8 + row)
            gs1_ref[at, :] = top * (sig * (1.0 + ema * (1.0 - sig)) * fall)
        return 0

    lax.fori_loop(0, HALF // 8, after1, 0)


def local_backward(half, carry_ref, par_ref, top_ref, gs1_ref, slope0_ref, power_ref, upper_ref, lower_ref, gs0_ref, hid_ref):
    lo = lower_lanes((8, LANES))
    fall_end = jnp.broadcast_to(power_ref[2 * HALF - 1 : 2 * HALF, :], (8, LANES))

    def wide(tile, row):
        return pl.ds(pl.multiple_of(tile * LANES + 16 * row + 8 * half, 8), 8)

    def narrow(tile, row):
        return pl.ds(pl.multiple_of(tile * HALF + 8 * row, 8), 8)

    def out_rows(tile, row):
        return pl.ds(tile * HALF + row, 8, stride=8)

    def entering(k, upper):
        even = carry_ref[pl.ds(8 * half * 16 + k, 8, stride=16), :]
        odd = carry_ref[pl.ds(8 * half * 16 + 8 + k, 8, stride=16), :]
        if upper:
            return jnp.where(lo, swap_halves(even), odd)
        return jnp.where(lo, even, swap_halves(odd))

    def rates(section, which):
        start = which * LANES + half * HALF
        return [par_ref[section, pl.ds(start + k, 8, stride=8), :] for k in range(K)]

    q1, w1, q0, w0 = (rates(section, which) for section in (1, 0) for which in (0, 1))
    last = HALF // 8 - 1

    def advance(state, qs, ws, lifted, tile, row):
        total = None
        for k in range(K):
            state[k] = state[k] * qs[k] + lifted
            term = state[k] * ws[k]
            total = term if total is None else total + term
        return total * jnp.broadcast_to(power_ref[pl.ds(tile * 8 + row, 1), :], (8, LANES))

    def upper(state, tile, row):
        at = wide(tile, row)
        grad = top_ref[at, :] + advance(state, q1, w1, gs1_ref[at, :], tile, row)
        upper_ref[out_rows(tile, row), :] = grad
        hid_ref[narrow(tile, row), :] = grad
        gs0_ref[narrow(tile, row), :] = grad * slope0_ref[at, :]

    def lower(state, tile, row):
        at = narrow(tile, row)
        lower_ref[out_rows(tile, row), :] = hid_ref[at, :] + advance(state, q0, w0, gs0_ref[at, :], tile, row)

    above = [entering(k, False) * fall_end for k in range(K)]
    below = [entering(k, True) * fall_end for k in range(K)]
    for row in range(7, -1, -1):
        upper(above, last, row)

    def step(it, state):
        above, below = list(state[:K]), list(state[K:])
        tile = last - 1 - it
        for row in range(7, -1, -1):
            upper(above, tile, row)
            lower(below, tile + 1, row)
        return tuple(above + below)

    below = list(lax.fori_loop(0, last, step, tuple(above + below)))[K:]
    for row in range(7, -1, -1):
        lower(below, 0, row)


def by_core(half, ins, keep_ref, send_ref, scratches):
    core = lax.axis_index("sect")

    @pl.when(core == 0)
    def _():
        local_backward(half, *ins, send_ref, keep_ref, *scratches)

    @pl.when(core == 1)
    def _():
        local_backward(half, *ins, keep_ref, send_ref, *scratches)


def first_half_kernel(*refs):
    ins, (own_ref, *others), (keep_ref, send_ref, mine_ref), scratches = refs[:6], refs[6:10], refs[10:13], refs[13:]
    own, xor1, xor2, xor3 = (ref[0:16, :] for ref in (own_ref, *others))
    total = (own + xor1) + (xor2 + xor3)
    mine_ref[...] = total[0:8, :]
    rows = keep_ref.shape[0]
    send_ref[rows : rows + 8, :] = total[8:16, :]
    by_core(0, ins, keep_ref, send_ref, scratches)


def second_half_kernel(*refs):
    ins, keep0_ref, (keep_ref, send_ref, out_hbm), scratches, sems = refs[:6], refs[6], refs[7:10], refs[10:12], refs[12]
    copies = half_copies(keep0_ref, out_hbm, lax.axis_index("sect"), 0, sems, 0)
    for copy in copies:
        copy.start()
    by_core(1, ins, keep_ref, send_ref, scratches)
    for copy in copies:
        copy.wait()


def half_copies(ref, out_hbm, slot, half, sems, first):
    return [
        pltpu.make_async_copy(
            ref.at[pl.ds(i * HALF, HALF)], out_hbm.at[slot, i, pl.ds(half * HALF, HALF)], sems.at[first + i]
        )
        for i in range(8)
    ]


def place_kernel(
    keep1_ref,
    recv_ref,
    mine_ref,
    scale_ref,
    placed_hbm,
    out_hbm,
    beta_hbm,
    eta_hbm,
    beta_ref,
    eta_ref,
    sems,
):
    del placed_hbm
    core = lax.axis_index("sect")
    copies = half_copies(recv_ref, out_hbm, 1 - core, 0, sems, 0)
    copies += half_copies(keep1_ref, out_hbm, core, 1, sems, 8)
    for copy in copies:
        copy.start()
    rows = keep1_ref.shape[0]
    total = mine_ref[...] + recv_ref[rows : rows + 8, :]
    beta_ref[...] = (scale_ref[0:8, :] * total)[:, :HALF]
    eta_ref[...] = (scale_ref[8:16, :] * total)[:, :HALF]
    small = [
        pltpu.make_async_copy(beta_ref, beta_hbm, sems.at[16]),
        pltpu.make_async_copy(eta_ref, eta_hbm, sems.at[17]),
    ]
    for copy in small:
        copy.start()
    for copy in copies + small:
        copy.wait()


def finish_kernel(recv_ref, placed_hbm, out_hbm, sems):
    del placed_hbm
    copies = half_copies(recv_ref, out_hbm, 1 - lax.axis_index("sect"), 1, sems, 0)
    for copy in copies:
        copy.start()
    for copy in copies:
        copy.wait()


def vmem():
    return pl.BlockSpec(memory_space=pltpu.VMEM)


def smem():
    return pl.BlockSpec(memory_space=pltpu.SMEM)


def hbm():
    return pl.BlockSpec(memory_space=pltpu.HBM)


def held(*dims):
    return vmem(), pltpu.VMEM(dims, F32)


def stored(*dims):
    return hbm(), pltpu.HBM(dims, F32)


def scratch(*dims):
    return pltpu.VMEM(dims, F32)


def run(kernel, name, ins, outs, scratches, args, aliases=None, limit=VMEM_LIMIT):
    return pl.pallas_call(
        kernel,
        in_specs=ins,
        out_specs=[spec for spec, _ in outs],
        out_shape=[shape for _, shape in outs],
        scratch_shapes=scratches,
        input_output_aliases=aliases or {},
        compiler_params=pltpu.CompilerParams(vmem_limit_bytes=limit),
        cost_estimate=pl.CostEstimate(flops=1_000, bytes_accessed=1_000, transcendentals=0),
        name=name,
    )(*args)


def per_device(
    features, rewards, done_flags, traj_len, decay_rate, input_gain, output_gain, value_head
):
    micro_rows, steps_local, width = features.shape
    rows = CHUNK * BLOCKS
    tiles = width // LANES
    swap = [(0, 1), (1, 0)]

    def out(*dims):
        return vmem(), jax.ShapeDtypeStruct(dims, F32)

    def exchange(a, per_block):
        return lax.all_to_all(a, "ctx", 0, 0).reshape(BLOCKS * per_block, LANES)

    (sent,) = run(
        pack_kernel,
        "pack",
        [hbm(), hbm()],
        [stored(BLOCKS * (CHUNK + 1), LANES)],
        [
            scratch(steps_local, width),
            pltpu.VMEM((micro_rows, steps_local), jnp.int32),
            scratch(BLOCKS * (CHUNK + 1), LANES),
            pltpu.SemaphoreType.DMA((9,)),
        ],
        (
            pltpu.with_memory_space_constraint(features, pltpu.HBM),
            pltpu.with_memory_space_constraint(done_flags, pltpu.HBM),
        ),
    )
    received = lax.all_to_all(sent.reshape(BLOCKS, CHUNK + 1, 1, LANES), "ctx", 0, 0)
    received = received.reshape(BLOCKS * (CHUNK + 1), LANES)
    own, gain = run(
        rates_kernel,
        "rates",
        [vmem()] * 3,
        [out(2 * K, width), out(2 * K, width)],
        [],
        (-jnp.expm1(-decay_rate[0]), input_gain[0], output_gain[0]),
    )
    other = lax.ppermute(own, "sect", swap)
    head = value_head.reshape(1, width)
    aux, par, scale, power = run(
        tables_kernel,
        "tables",
        [smem()] * 2 + [vmem()] * 5,
        [
            out(AUX_ROWS, LANES),
            out(2, 2 * LANES, LANES),
            out(2 * K, LANES),
            out(2 * HALF, LANES),
        ],
        [],
        (traj_len, done_flags, own, other, gain, head, rewards),
    )
    sent_values, lift0, lift1, slope0, slope1, end0, flags, falls, rise = run(
        forward_kernel,
        "forward",
        [vmem()] * 2,
        [held(BLOCKS * PAYLOAD, LANES)]
        + [held(rows, LANES)] * 4
        + [held(K * 32, LANES)]
        + [held(BLOCKS, LANES)] * 2
        + [held(rows, LANES)],
        [scratch(rows, LANES)] * 3 + [scratch(K * 32, LANES)] * 4,
        (received, aux),
    )
    values = exchange(sent_values.reshape(BLOCKS, PAYLOAD, LANES), PAYLOAD)
    sent_carries, small = run(
        backward_kernel,
        "backward",
        [vmem()] * 10,
        [stored(BLOCKS, K, LANES), held(3 * K, LANES)],
        [scratch(rows, LANES)] * 2
        + [scratch(K * 32, LANES)] * 4
        + [scratch(BLOCKS, K, LANES), scratch(BLOCKS, LANES), pltpu.SemaphoreType.DMA((4,))],
        (values, aux, flags, falls, lift0, lift1, slope0, slope1, end0, rise),
    )
    carries = exchange(sent_carries, K)
    others = [lax.ppermute(small, "dp", [(i, i ^ far) for i in range(4)]) for far in (1, 2, 3)]
    by_tile = (
        features.reshape(micro_rows, steps_local // 8, 8, tiles, LANES)
        .transpose(0, 1, 3, 2, 4)
        .reshape(micro_rows, rows, LANES)
    )
    top, local_gs1, local_slope0 = run(
        local_forward_kernel,
        "local_forward",
        [vmem()] * 6,
        [out(rows, LANES)] * 3,
        [scratch(rows, LANES)] * 2 + [scratch(HALF, LANES)],
        (small, by_tile, values, par, power, value_head.reshape(tiles, LANES)),
    )
    local = (carries, par, top, local_gs1, local_slope0, power)
    half_rows = rows // 2
    keep0, send0, mine = run(
        first_half_kernel,
        "local_backward0",
        [vmem()] * 10,
        [out(half_rows, LANES), out(half_rows + 8, LANES), out(K, LANES)],
        [scratch(half_rows, LANES)] * 2,
        (*local, small, *others),
    )
    swapped0 = lax.ppermute(send0, "sect", swap)
    keep1, send1, placed0 = run(
        second_half_kernel,
        "local_backward1",
        [vmem()] * 7,
        [out(half_rows, LANES), out(half_rows, LANES), stored(2, 8, LANES, LANES)],
        [scratch(half_rows, LANES)] * 2 + [pltpu.SemaphoreType.DMA((8,))],
        (*local, keep0),
    )
    swapped1 = lax.ppermute(send1, "sect", swap)
    placed, grad_beta, grad_eta = run(
        place_kernel,
        "place",
        [vmem()] * 4 + [hbm()],
        [stored(2, 8, LANES, LANES), stored(K, HALF), stored(K, HALF)],
        [scratch(K, HALF)] * 2 + [pltpu.SemaphoreType.DMA((18,))],
        (keep1, swapped0, mine, scale, placed0),
        {4: 0},
    )
    (grads,) = run(
        finish_kernel,
        "finish",
        [vmem(), hbm()],
        [stored(2, 8, LANES, LANES)],
        [pltpu.SemaphoreType.DMA((8,))],
        (swapped1, placed),
        {1: 0},
    )
    grad_inputs = (
        grads.reshape(micro_rows, steps_local // 8, tiles, 8, LANES)
        .transpose(0, 1, 3, 2, 4)
        .reshape(1, micro_rows, steps_local, width)
    )
    return (grad_inputs, grad_beta[None], grad_eta[None])


def solution(mesh):
    placed = (
        P("dp", "ctx", None),
        P("dp", "ctx"),
        P("dp", "ctx"),
        P(),
        P("sect", None, None),
        P("sect", None, None),
        P("sect", None, None),
        P(),
    )
    return jax.shard_map(
        per_device,
        mesh=mesh,
        in_specs=placed,
        out_specs=(P("sect", "dp", "ctx", None), P("sect", None, "ctx"), P("sect", None, "ctx")),
        check_vma=False,
    )
```

```python
import math

import jax
import jax.numpy as jnp
from jax import lax
from jax.experimental import pallas as pl
from jax.experimental.pallas import tpu as pltpu
from jax.sharding import PartitionSpec as P

F32 = jnp.float32
LANES = 128
K = 8
HALF = 64
UNROLL = 8
CHUNK = 32
BLOCKS = 32
VMEM_LIMIT = 12 * 1024 * 1024
AUX_ROWS = 64


def lane_index(shape):
    return lax.broadcasted_iota(jnp.int32, shape, len(shape) - 1)


def lower_lanes(shape):
    return lane_index(shape) < HALF


def swap_halves(a):
    return pltpu.roll(a, HALF, 1)


def gather_lanes(a, lanes):
    return jnp.take_along_axis(a, lanes, axis=1, mode="promise_in_bounds")


def token_lanes():
    return jnp.where(lower_lanes((8, LANES)), 0, CHUNK)


def sigmoid(v):
    return 0.5 * jnp.tanh(0.5 * v) + 0.5


def rows_of(ref, start, stride, size=8):
    return ref[pl.ds(start, size, stride=stride), :]


def pack_kernel(feat_hbm, flag_hbm, out_hbm, feat_ref, flag_ref, out_ref, sems):
    core = lax.axis_index("sect")
    parts = 4
    wide = feat_ref.shape[1] // parts
    tall = out_ref.shape[0] // parts
    flag_copy = pltpu.make_async_copy(flag_hbm, flag_ref, sems.at[2 * parts])
    flag_copy.start()
    arriving, leaving = [], []
    for part in range(parts):
        lanes, rows = pl.ds(part * wide, wide), pl.ds(part * tall, tall)
        arriving.append(
            pltpu.make_async_copy(feat_hbm.at[core, :, lanes], feat_ref.at[:, lanes], sems.at[part])
        )
        leaving.append(
            pltpu.make_async_copy(out_ref.at[rows], out_hbm.at[rows], sems.at[parts + part])
        )
        arriving[-1].start()
    lo = lower_lanes((8, LANES))
    flag_copy.wait()
    flags = flag_ref[pl.ds(core, 1), :].astype(F32)
    row = jnp.concatenate([flags, jnp.zeros((1, HALF), F32)], axis=1)
    for block in range(BLOCKS):
        at = block * (CHUNK + 1) + CHUNK
        out_ref[at : at + 1, :] = row
    for part in range(parts):
        arriving[part].wait()
        for pair in range(part * BLOCKS // (2 * parts), (part + 1) * BLOCKS // (2 * parts)):
            for g in range(CHUNK // 8):
                lanes = slice(pair * LANES, (pair + 1) * LANES)
                early = feat_ref[8 * g : 8 * g + 8, lanes]
                late = feat_ref[CHUNK + 8 * g : CHUNK + 8 * g + 8, lanes]
                even_row = 2 * pair * (CHUNK + 1) + 8 * g
                odd_row = (2 * pair + 1) * (CHUNK + 1) + 8 * g
                out_ref[even_row : even_row + 8, :] = jnp.where(lo, early, swap_halves(late))
                out_ref[odd_row : odd_row + 8, :] = jnp.where(lo, swap_halves(early), late)
        leaving[part].start()
    for copy in leaving:
        copy.wait()


def rates_kernel(p_ref, beta_ref, eta_ref, own_ref, gain_ref):
    p = p_ref[...]
    scale = jnp.sqrt(p * (2.0 - p))
    in_scale = scale * beta_ref[...]
    own_ref[0:8, :] = 1.0 - p
    own_ref[8:16, :] = in_scale * eta_ref[...]
    gain_ref[0:8, :] = scale * eta_ref[...]
    gain_ref[8:16, :] = in_scale


def channel_tile(ref, place, lo_row, rows):
    start = pl.multiple_of((place // 2) * LANES, LANES)
    tile = ref[lo_row : lo_row + rows, pl.ds(start, LANES)]
    flipped = swap_halves(tile)
    lo = lower_lanes((rows, LANES))
    odd = (place % 2) == 1
    return jnp.where(odd, jnp.where(lo, flipped, tile), jnp.where(lo, tile, flipped))


def tables_kernel(
    lens_ref,
    flag_ref,
    own_ref,
    other_ref,
    gain_ref,
    head_ref,
    rewards_ref,
    aux_ref,
    par_ref,
    scale_ref,
    power_ref,
):
    core, place, dp = lax.axis_index("sect"), lax.axis_index("ctx"), lax.axis_index("dp")
    for section in range(2):
        here = core == section
        q = jnp.where(here, channel_tile(own_ref, place, 0, 8), channel_tile(other_ref, place, 0, 8))
        w = jnp.where(here, channel_tile(own_ref, place, 8, 8), channel_tile(other_ref, place, 8, 8))
        aux_ref[16 * section : 16 * section + 8, :] = q
        aux_ref[16 * section + 8 : 16 * section + 16, :] = w
        aux_ref[32 + 8 * section : 40 + 8 * section, :] = power32(q)
        for which in range(2):
            for tile in range(16):
                rows, lanes = slice(8 * which, 8 * which + 8), slice(tile * LANES, (tile + 1) * LANES)
                at = which * LANES + tile * 8
                par_ref[section, at : at + 8, :] = jnp.where(here, own_ref[rows, lanes], other_ref[rows, lanes])
    aux_ref[48:56, :] = jnp.broadcast_to(channel_tile(head_ref, place, 0, 1), (8, LANES))
    rewards = rewards_ref[pl.ds(core, 1), :]
    aux_ref[56:57, :] = jnp.concatenate([rewards, jnp.zeros((1, HALF), F32)], axis=1)
    aux_ref[57:64, :] = jnp.full((7, LANES), lens_ref[dp * 2 + core].astype(F32))
    scale_ref[...] = channel_tile(gain_ref, place, 0, 16)
    rise = jnp.float32(1.0)
    fall = jnp.float32(1.0)
    for t in range(HALF):
        flag = flag_ref[core, t].astype(F32)
        rise = rise * (1.0 + flag)
        fall = fall * (1.0 - 0.5 * flag)
        power_ref[t : t + 1, :] = jnp.full((1, LANES), rise)
        power_ref[HALF + t : HALF + t + 1, :] = jnp.full((1, LANES), fall)


def power32(q):
    for _ in range(5):
        q = q * q
    return q


def spread(a, k):
    return jnp.broadcast_to(a[k : k + 1, :], (8, LANES))


def ends_pass(lifted_ref, q, store_end):
    qs = [spread(q, k) for k in range(K)]
    for pair in range(2):
        groups = (2 * pair, 2 * pair + 1)

        def step(it, state):
            state = list(state)
            for u in range(UNROLL):
                r = it * UNROLL + u
                for i, g in enumerate(groups):
                    lifted = lifted_ref[pl.ds(pl.multiple_of(r * 32 + 8 * g, 8), 8), :]
                    for k in range(K):
                        state[i * K + k] = state[i * K + k] * qs[k] + lifted
            return tuple(state)

        state = lax.fori_loop(0, CHUNK // UNROLL, step, tuple(jnp.zeros((8, LANES), F32) for _ in range(16)))
        for i, g in enumerate(groups):
            for k in range(K):
                store_end(k, g, state[i * K + k])


def at_row(r, g):
    return pl.ds(pl.multiple_of(r * 32 + 8 * g, 8), 8)


def halves_of(a):
    flipped = swap_halves(a)
    lo = lower_lanes(a.shape)
    return jnp.where(lo, a, flipped), jnp.where(lo, flipped, a)


def forward_carries(end_ref, fall_ref, q32, carry_ref, in_ref):
    lo = lower_lanes((8, LANES))
    q64 = q32 * q32
    carry = jnp.zeros((8, LANES), F32)
    for block in range(BLOCKS):
        end_early, end_late = halves_of(rows_of(end_ref, block, 32))
        fall_early, fall_late = halves_of(fall_ref[block : block + 1, :])
        entering_late = q32 * fall_early * carry + end_early
        carry_ref[block * 8 : block * 8 + 8, :] = carry
        in_ref[pl.ds(block, 8, stride=32), :] = jnp.where(lo, carry, entering_late)
        block_end = q32 * fall_late * end_early + end_late
        carry = q64 * (fall_early * fall_late) * carry + block_end


def forward_pass(lifted_ref, fall_ref, in_ref, q, w, ema_ref):
    qs = [spread(q, k) for k in range(K)]
    ws = [spread(w, k) for k in range(K)]
    for pair in range(2):
        groups = (2 * pair, 2 * pair + 1)

        def step(it, state):
            state = list(state)
            for u in range(UNROLL):
                r = it * UNROLL + u
                for i, g in enumerate(groups):
                    at = pl.ds(pl.multiple_of(r * 32 + 8 * g, 8), 8)
                    lifted = lifted_ref[at, :]
                    total = None
                    for k in range(K):
                        new = state[i * K + k] * qs[k] + lifted
                        state[i * K + k] = new
                        term = new * ws[k]
                        total = term if total is None else total + term
                    ema_ref[at, :] = total * fall_ref[at, :]
            return tuple(state)

        start = tuple(in_ref[k * 32 + 8 * g : k * 32 + 8 * g + 8, :] for g in groups for k in range(K))
        lax.fori_loop(0, CHUNK // UNROLL, step, start)


def lane_sums(vectors, bits):
    lane = lane_index((8, LANES))
    for bit in bits:
        mask = (lane & (1 << bit)) == 0
        pairs = [(vectors[2 * m], vectors[2 * m + 1]) for m in range(len(vectors) // 2)]
        vectors = [
            jnp.where(mask, a, b) + gather_lanes(jnp.where(mask, b, a), lane ^ (1 << bit))
            for a, b in pairs
        ]
    return vectors[0]


def last_lane_sums(vectors):
    lane = lane_index((8, LANES))
    v = lane_sums(vectors, (3, 4))
    v = v + gather_lanes(v, lane ^ 32)
    return jnp.where(lane < CHUNK, v, pltpu.roll(v, LANES - CHUNK, 1))


PAYLOAD = BLOCKS // 2 + K


def forward_kernel(
    recv_ref,
    aux_ref,
    out_ref,
    lift0_ref,
    lift1_ref,
    slope0_ref,
    slope1_ref,
    end0_ref,
    flags_ref,
    falls_ref,
    rise_ref,
    fall_ref,
    ema_ref,
    hid_ref,
    end1_ref,
    in_ref,
    carry0_ref,
    carry1_ref,
):
    place = lax.axis_index("ctx")
    stride = CHUNK + 1
    q0, w0, q1, w1 = (aux_ref[8 * i : 8 * i + 8, :] for i in range(4))
    lo = lower_lanes((8, LANES))
    lanes = token_lanes()

    for g in range(4):
        flags = rows_of(recv_ref, 8 * g * stride + CHUNK, stride)
        flags_ref[8 * g : 8 * g + 8, :] = flags
        rise = jnp.ones((8, LANES), F32)
        fall = jnp.ones((8, LANES), F32)
        for r in range(CHUNK):
            flag = gather_lanes(flags, lanes + r)
            rise = rise * (1.0 + flag)
            fall = fall * (1.0 - 0.5 * flag)
            at = slice(r * 32 + 8 * g, r * 32 + 8 * g + 8)
            rise_ref[at, :] = rise
            fall_ref[at, :] = fall
            lift0_ref[at, :] = rows_of(recv_ref, 8 * g * stride + r, stride) * rise
        falls_ref[8 * g : 8 * g + 8, :] = fall

    def store(end_ref):
        def one(k, g, u):
            at = slice(k * 32 + 8 * g, k * 32 + 8 * g + 8)
            end_ref[at, :] = u * falls_ref[8 * g : 8 * g + 8, :]

        return one

    ends_pass(lift0_ref, q0, store(end0_ref))
    forward_carries(end0_ref, falls_ref, aux_ref[32:40, :], carry0_ref, in_ref)
    forward_pass(lift0_ref, fall_ref, in_ref, q0, w0, ema_ref)

    def after0(it, _):
        for u in range(8):
            at = pl.ds(pl.multiple_of(it * 64 + 8 * u, 8), 8)
            ema, fall = ema_ref[at, :], fall_ref[at, :]
            sig = sigmoid(ema)
            hidden = lift0_ref[at, :] * fall + ema * sig
            hid_ref[at, :] = hidden
            lift1_ref[at, :] = hidden * rise_ref[at, :]
            slope0_ref[at, :] = sig * (1.0 + ema * (1.0 - sig)) * fall
        return 0

    lax.fori_loop(0, 16, after0, 0)
    ends_pass(lift1_ref, q1, store(end1_ref))
    forward_carries(end1_ref, falls_ref, aux_ref[40:48, :], carry1_ref, in_ref)
    forward_pass(lift1_ref, fall_ref, in_ref, q1, w1, ema_ref)
    head8 = aux_ref[48:56, :]

    parts = []
    for g in range(4):
        for first in range(0, CHUNK, 8):
            tops = []
            for r in range(first, first + 8):
                at = slice(r * 32 + 8 * g, r * 32 + 8 * g + 8)
                ema = ema_ref[at, :]
                sig = sigmoid(ema)
                slope1_ref[at, :] = sig * (1.0 + ema * (1.0 - sig)) * fall_ref[at, :]
                tops.append((hid_ref[at, :] + ema * sig) * head8)
            parts.append(lane_sums(tops, (0, 1, 2)))
    values = jnp.concatenate([last_lane_sums(parts[4 * g : 4 * g + 4]) for g in range(4)], axis=0)
    total = BLOCKS * HALF
    gamma = math.exp(-0.25 / total)
    shape = (BLOCKS, LANES)
    lane = lane_index(shape)
    row = lax.broadcasted_iota(jnp.int32, shape, 0)
    after = (row * HALF + lane + 1).astype(F32)
    next_block = pltpu.roll(pltpu.roll(values, BLOCKS - 1, 0), HALF - 1, 1)
    following = jnp.where(lane == HALF - 1, next_block, pltpu.roll(values, LANES - 1, 1))
    following = jnp.where(after < aux_ref[57:58, :], following, 0.0)
    part = gamma * (1.0 - flags_ref[...]) * following - values
    part = part + jnp.where(row == place, aux_ref[56:57, :], 0.0)
    half_rows = BLOCKS // 2
    packed = jnp.where(
        lower_lanes((half_rows, LANES)), part[:half_rows, :], swap_halves(part[half_rows:, :])
    )
    for block in range(BLOCKS):
        at = block * PAYLOAD
        rows = slice(block * 8, block * 8 + 8)
        out_ref[at : at + half_rows, :] = packed
        out_ref[at + half_rows : at + PAYLOAD, :] = jnp.where(lo, carry0_ref[rows, :], carry1_ref[rows, :])


def starts_pass(grad_ref, q, start_ref, lift_ref=None):
    qs = [spread(q, k) for k in range(K)]
    sums = [jnp.zeros((8, LANES), F32) for _ in range(K)]
    for pair in range(2):
        groups = (2 * pair, 2 * pair + 1)

        def step(it, state):
            state = list(state)
            for u in range(UNROLL):
                r = CHUNK - 1 - (it * UNROLL + u)
                for i, g in enumerate(groups):
                    grad = grad_ref[at_row(r, g), :]
                    lifted = None if lift_ref is None else lift_ref[at_row(r, g), :]
                    for k in range(K):
                        new = state[i * K + k] * qs[k] + grad
                        state[i * K + k] = new
                        if lift_ref is not None:
                            state[16 + k] = state[16 + k] + new * lifted
            return tuple(state)

        begin = [jnp.zeros((8, LANES), F32) for _ in range(16)]
        if lift_ref is not None:
            begin = begin + sums
        state = lax.fori_loop(0, CHUNK // UNROLL, step, tuple(begin))
        sums = list(state[16:])
        for i, g in enumerate(groups):
            for k in range(K):
                start_ref[k * 32 + 8 * g : k * 32 + 8 * g + 8, :] = state[i * K + k]
    return sums


def backward_carries(start_ref, fall_ref, q32, carry_ref, in_ref=None, end_ref=None, entered=None):
    lo = lower_lanes((8, LANES))
    q64 = q32 * q32
    carry = jnp.zeros((8, LANES), F32)
    added = jnp.zeros((8, LANES), F32)
    for block in range(BLOCKS - 1, -1, -1):
        start_early, start_late = halves_of(rows_of(start_ref, block, 32))
        fall_early, fall_late = halves_of(fall_ref[block : block + 1, :])
        entering_early = q32 * fall_late * carry + start_late
        carry_ref[block * 8 : block * 8 + 8, :] = carry
        if entered is not None:
            entered(block, carry)
        entering = jnp.where(lo, entering_early, carry)
        if in_ref is not None:
            in_ref[pl.ds(block, 8, stride=32), :] = entering * fall_ref[block : block + 1, :]
        if end_ref is not None:
            added = added + entering * rows_of(end_ref, block, 32)
        block_start = q32 * fall_early * start_late + start_early
        carry = q64 * (fall_early * fall_late) * carry + block_start
    return added


def backward_pass(grad_ref, top_ref, rise_ref, slope_ref, lift_ref, in_ref, q, w, out_ref):
    qs = [spread(q, k) for k in range(K)]
    ws = [spread(w, k) for k in range(K)]
    sums = [jnp.zeros((8, LANES), F32) for _ in range(K)]
    for pair in range(2):
        groups = (2 * pair, 2 * pair + 1)

        def step(it, state):
            state = list(state)
            for u in range(UNROLL):
                r = CHUNK - 1 - (it * UNROLL + u)
                for i, g in enumerate(groups):
                    at = pl.ds(pl.multiple_of(r * 32 + 8 * g, 8), 8)
                    grad = grad_ref[at, :]
                    lifted = lift_ref[at, :]
                    total = None
                    for k in range(K):
                        new = state[i * K + k] * qs[k] + grad
                        state[i * K + k] = new
                        state[16 + k] = state[16 + k] + new * lifted
                        term = new * ws[k]
                        total = term if total is None else total + term
                    out_ref[at, :] = (top_ref[at, :] + rise_ref[at, :] * total) * slope_ref[at, :]
            return tuple(state)

        start = [in_ref[k * 32 + 8 * g : k * 32 + 8 * g + 8, :] for g in groups for k in range(K)]
        state = lax.fori_loop(0, CHUNK // UNROLL, step, tuple(start + sums))
        sums = list(state[16:])
    return sums


def folded(sums):
    return jnp.concatenate([jnp.sum(a, axis=0, keepdims=True) for a in sums], axis=0)


def four_steps(summed, reach, s, axis, index, limit):
    size = summed.shape[axis]

    def later(a, m, beyond):
        return jnp.where(index + m * s < limit, pltpu.roll(a, size - m * s, axis), beyond)

    a1, a2, a3 = (later(summed, m, 0.0) for m in (1, 2, 3))
    r1, r2, r3 = (later(reach, m, 1.0) for m in (1, 2, 3))
    near, far = reach * r1, r2 * r3
    return (summed + reach * a1) + near * (a2 + r2 * a3), near * far


def backward_kernel(
    td_ref,
    aux_ref,
    flags_ref,
    falls_ref,
    lift0_ref,
    lift1_ref,
    slope0_ref,
    slope1_ref,
    end0_ref,
    rise_ref,
    out_hbm,
    small_ref,
    gs_ref,
    top_ref,
    start_ref,
    back0_ref,
    back1_ref,
    in_ref,
    both_ref,
    all_ref,
    sems,
):
    core, place = lax.axis_index("sect"), lax.axis_index("ctx")
    q0, w0, q1, w1 = (aux_ref[8 * i : 8 * i + 8, :] for i in range(4))
    half_rows = BLOCKS // 2
    packed = td_ref[0:half_rows, :]
    for block in range(1, BLOCKS):
        packed = packed + td_ref[block * PAYLOAD : block * PAYLOAD + half_rows, :]
    total = BLOCKS * HALF
    trace = math.exp(-1.0 / total)
    shape = (BLOCKS, LANES)
    lane = lane_index(shape)
    row = lax.broadcasted_iota(jnp.int32, shape, 0)
    valid = ((row * HALF + lane).astype(F32) < aux_ref[57:58, :]) & (lane < HALF)
    td = jnp.where(valid, jnp.concatenate([packed, swap_halves(packed)], axis=0), 0.0)
    reach = trace * (1.0 - flags_ref[...])
    adv = td
    for s in (1, 4, 16):
        adv, reach = four_steps(adv, reach, s, 1, lane, HALF)
    block_adv = jnp.broadcast_to(adv[:, 0:1], shape)
    block_reach = jnp.broadcast_to(reach[:, 0:1], shape)
    for s in (1, 4):
        block_adv, block_reach = four_steps(block_adv, block_reach, s, 0, row, BLOCKS)
    block_adv = block_adv + block_reach * jnp.where(row < 16, pltpu.roll(block_adv, 16, 0), 0.0)
    arriving = jnp.where(row + 1 < BLOCKS, pltpu.roll(block_adv, BLOCKS - 1, 0), 0.0)
    grad = jnp.where(valid, -(adv + reach * arriving), 0.0)
    all_ref[...] = grad
    small_ref[16:24, :] = jnp.broadcast_to(all_ref[pl.ds(place, 1), :], (8, LANES))

    head8 = aux_ref[48:56, :]
    lo = lower_lanes((8, LANES))
    lanes = token_lanes()
    for g in range(4):
        rows = grad[8 * g : 8 * g + 8, :]
        for r in range(CHUNK):
            at = slice(r * 32 + 8 * g, r * 32 + 8 * g + 8)
            top = gather_lanes(rows, lanes + r) * head8
            top_ref[at, :] = top
            gs_ref[at, :] = top * slope1_ref[at, :]

    starts_pass(gs_ref, q1, start_ref)
    backward_carries(start_ref, falls_ref, aux_ref[40:48, :], back1_ref, in_ref)
    sums1 = backward_pass(gs_ref, top_ref, rise_ref, slope0_ref, lift1_ref, in_ref, q1, w1, gs_ref)
    sums0 = starts_pass(gs_ref, q0, start_ref, lift0_ref)
    copies = []

    def entered(block, carry):
        both_ref[block] = jnp.where(lo, back1_ref[block * 8 : block * 8 + 8, :], carry)
        if block % 8 == 0:
            piece = pl.ds(block, 8)
            copies.append(
                pltpu.make_async_copy(both_ref.at[piece], out_hbm.at[piece], sems.at[block // 8])
            )
            copies[-1].start()

    added0 = backward_carries(
        start_ref, falls_ref, aux_ref[32:40, :], back0_ref, None, end0_ref, entered
    )
    full0 = folded(sums0) + q0 * added0
    full1 = folded(sums1)
    full0 = full0 + swap_halves(full0)
    full1 = full1 + swap_halves(full1)
    first = core == 0
    small_ref[0:8, :] = jnp.where(first, full0, full1)
    small_ref[8:16, :] = jnp.where(first, full1, full0)
    for copy in copies:
        copy.wait()


def carried(carry_ref, k, rows, base, upper):
    lo = lower_lanes((16, LANES))
    even = carry_ref[pl.ds(base + k, 16, stride=2 * rows), :]
    odd = carry_ref[pl.ds(rows + base + k, 16, stride=2 * rows), :]
    if upper:
        return jnp.where(lo, swap_halves(even), odd)
    return jnp.where(lo, even, swap_halves(odd))


def section_rates(par_ref, section, which):
    return [par_ref[section, pl.ds(which * LANES + k, 16, stride=8), :] for k in range(K)]


def local_forward_kernel(
    small_ref,
    feat_ref,
    carry_ref,
    par_ref,
    power_ref,
    head_ref,
    top_ref,
    gs1_ref,
    slope0_ref,
    ema_ref,
    hid_ref,
    grad_ref,
):
    core = lax.axis_index("sect")
    head = head_ref[...]
    row = small_ref[16:17, :]
    for t in range(HALF):
        grad_ref[t : t + 1, :] = jnp.broadcast_to(row[:, t : t + 1], (1, LANES))

    def across(ref, at):
        return jnp.broadcast_to(ref[pl.ds(at, 1), :], (16, LANES))

    def token(tile, row):
        return pl.ds(tile * LANES + row, 16, stride=8)

    def local(tile, row):
        return pl.ds(pl.multiple_of(tile * LANES + row * 16, 16), 16)

    def forward(section, read):
        qs, ws = section_rates(par_ref, section, 0), section_rates(par_ref, section, 1)

        def step(tile, state):
            state = list(state)
            for row in range(8):
                lifted = read(tile, row) * across(power_ref, tile * 8 + row)
                total = None
                for k in range(K):
                    state[k] = state[k] * qs[k] + lifted
                    term = state[k] * ws[k]
                    total = term if total is None else total + term
                ema_ref[local(tile, row), :] = total * across(power_ref, HALF + tile * 8 + row)
            return tuple(state)

        begin = tuple(carried(carry_ref, k, PAYLOAD, BLOCKS // 2, section == 1) for k in range(K))
        lax.fori_loop(0, HALF // 8, step, begin)

    forward(0, lambda *at: feat_ref[core, token(*at), :])

    def after0(tile, _):
        for row in range(8):
            at = local(tile, row)
            ema = ema_ref[at, :]
            sig = sigmoid(ema)
            hid_ref[at, :] = feat_ref[core, token(tile, row), :] + ema * sig
            fall = across(power_ref, HALF + tile * 8 + row)
            slope0_ref[at, :] = sig * (1.0 + ema * (1.0 - sig)) * fall
        return 0

    lax.fori_loop(0, HALF // 8, after0, 0)
    forward(1, lambda *at: hid_ref[local(*at), :])

    def after1(tile, _):
        for row in range(8):
            at = local(tile, row)
            ema = ema_ref[at, :]
            sig = sigmoid(ema)
            top = head * across(grad_ref, tile * 8 + row)
            top_ref[at, :] = top
            fall = across(power_ref, HALF + tile * 8 + row)
            gs1_ref[at, :] = top * (sig * (1.0 + ema * (1.0 - sig)) * fall)
        return 0

    lax.fori_loop(0, HALF // 8, after1, 0)


def local_backward(half, carry_ref, par_ref, top_ref, gs1_ref, slope0_ref, power_ref, upper_ref, lower_ref, gs0_ref, hid_ref):
    lo = lower_lanes((8, LANES))
    fall_end = jnp.broadcast_to(power_ref[2 * HALF - 1 : 2 * HALF, :], (8, LANES))

    def wide(tile, row):
        return pl.ds(pl.multiple_of(tile * LANES + 16 * row + 8 * half, 8), 8)

    def narrow(tile, row):
        return pl.ds(pl.multiple_of(tile * HALF + 8 * row, 8), 8)

    def out_rows(tile, row):
        return pl.ds(tile * HALF + row, 8, stride=8)

    def entering(k, upper):
        even = carry_ref[pl.ds(8 * half * 16 + k, 8, stride=16), :]
        odd = carry_ref[pl.ds(8 * half * 16 + 8 + k, 8, stride=16), :]
        if upper:
            return jnp.where(lo, swap_halves(even), odd)
        return jnp.where(lo, even, swap_halves(odd))

    def rates(section, which):
        start = which * LANES + half * HALF
        return [par_ref[section, pl.ds(start + k, 8, stride=8), :] for k in range(K)]

    q1, w1, q0, w0 = (rates(section, which) for section in (1, 0) for which in (0, 1))
    last = HALF // 8 - 1

    def advance(state, qs, ws, lifted, tile, row):
        total = None
        for k in range(K):
            state[k] = state[k] * qs[k] + lifted
            term = state[k] * ws[k]
            total = term if total is None else total + term
        return total * jnp.broadcast_to(power_ref[pl.ds(tile * 8 + row, 1), :], (8, LANES))

    def upper(state, tile, row):
        at = wide(tile, row)
        grad = top_ref[at, :] + advance(state, q1, w1, gs1_ref[at, :], tile, row)
        upper_ref[out_rows(tile, row), :] = grad
        hid_ref[narrow(tile, row), :] = grad
        gs0_ref[narrow(tile, row), :] = grad * slope0_ref[at, :]

    def lower(state, tile, row):
        at = narrow(tile, row)
        lower_ref[out_rows(tile, row), :] = hid_ref[at, :] + advance(state, q0, w0, gs0_ref[at, :], tile, row)

    above = [entering(k, False) * fall_end for k in range(K)]
    below = [entering(k, True) * fall_end for k in range(K)]
    for row in range(7, -1, -1):
        upper(above, last, row)

    def step(it, state):
        above, below = list(state[:K]), list(state[K:])
        tile = last - 1 - it
        for row in range(7, -1, -1):
            upper(above, tile, row)
            lower(below, tile + 1, row)
        return tuple(above + below)

    below = list(lax.fori_loop(0, last, step, tuple(above + below)))[K:]
    for row in range(7, -1, -1):
        lower(below, 0, row)


def by_core(half, ins, keep_ref, send_ref, scratches):
    core = lax.axis_index("sect")

    @pl.when(core == 0)
    def _():
        local_backward(half, *ins, send_ref, keep_ref, *scratches)

    @pl.when(core == 1)
    def _():
        local_backward(half, *ins, keep_ref, send_ref, *scratches)


def first_half_kernel(*refs):
    ins, (own_ref, *others), (keep_ref, send_ref, mine_ref), scratches = refs[:6], refs[6:10], refs[10:13], refs[13:]
    own, xor1, xor2, xor3 = (ref[0:16, :] for ref in (own_ref, *others))
    total = (own + xor1) + (xor2 + xor3)
    mine_ref[...] = total[0:8, :]
    rows = keep_ref.shape[0]
    send_ref[rows : rows + 8, :] = total[8:16, :]
    by_core(0, ins, keep_ref, send_ref, scratches)


def second_half_kernel(*refs):
    ins, keep0_ref, (keep_ref, send_ref, out_hbm), scratches, sems = refs[:6], refs[6], refs[7:10], refs[10:12], refs[12]
    copies = half_copies(keep0_ref, out_hbm, lax.axis_index("sect"), 0, sems, 0)
    for copy in copies:
        copy.start()
    by_core(1, ins, keep_ref, send_ref, scratches)
    for copy in copies:
        copy.wait()


def half_copies(ref, out_hbm, slot, half, sems, first):
    return [
        pltpu.make_async_copy(
            ref.at[pl.ds(i * HALF, HALF)], out_hbm.at[slot, i, pl.ds(half * HALF, HALF)], sems.at[first + i]
        )
        for i in range(8)
    ]


def place_kernel(
    keep1_ref,
    recv_ref,
    mine_ref,
    scale_ref,
    placed_hbm,
    out_hbm,
    beta_hbm,
    eta_hbm,
    beta_ref,
    eta_ref,
    sems,
):
    del placed_hbm
    core = lax.axis_index("sect")
    copies = half_copies(recv_ref, out_hbm, 1 - core, 0, sems, 0)
    copies += half_copies(keep1_ref, out_hbm, core, 1, sems, 8)
    for copy in copies:
        copy.start()
    rows = keep1_ref.shape[0]
    total = mine_ref[...] + recv_ref[rows : rows + 8, :]
    beta_ref[...] = (scale_ref[0:8, :] * total)[:, :HALF]
    eta_ref[...] = (scale_ref[8:16, :] * total)[:, :HALF]
    small = [
        pltpu.make_async_copy(beta_ref, beta_hbm, sems.at[16]),
        pltpu.make_async_copy(eta_ref, eta_hbm, sems.at[17]),
    ]
    for copy in small:
        copy.start()
    for copy in copies + small:
        copy.wait()


def finish_kernel(recv_ref, placed_hbm, out_hbm, sems):
    del placed_hbm
    core = lax.axis_index("sect")
    copies = [
        pltpu.make_async_copy(
            recv_ref.at[pl.ds(4 * i, 4)],
            out_hbm.at[1 - core, pl.ds(4 * i, 4), pl.ds(HALF, HALF)],
            sems.at[i],
        )
        for i in range(2)
    ]
    for copy in copies:
        copy.start()
    for copy in copies:
        copy.wait()


def vmem():
    return pl.BlockSpec(memory_space=pltpu.VMEM)


def smem():
    return pl.BlockSpec(memory_space=pltpu.SMEM)


def hbm():
    return pl.BlockSpec(memory_space=pltpu.HBM)


def held(*dims):
    return vmem(), pltpu.VMEM(dims, F32)


def stored(*dims):
    return hbm(), pltpu.HBM(dims, F32)


def scratch(*dims):
    return pltpu.VMEM(dims, F32)


def run(kernel, name, ins, outs, scratches, args, aliases=None, limit=VMEM_LIMIT):
    return pl.pallas_call(
        kernel,
        in_specs=ins,
        out_specs=[spec for spec, _ in outs],
        out_shape=[shape for _, shape in outs],
        scratch_shapes=scratches,
        input_output_aliases=aliases or {},
        compiler_params=pltpu.CompilerParams(vmem_limit_bytes=limit),
        cost_estimate=pl.CostEstimate(flops=1_000, bytes_accessed=1_000, transcendentals=0),
        name=name,
    )(*args)


def per_device(
    features, rewards, done_flags, traj_len, decay_rate, input_gain, output_gain, value_head
):
    micro_rows, steps_local, width = features.shape
    rows = CHUNK * BLOCKS
    tiles = width // LANES
    swap = [(0, 1), (1, 0)]

    def out(*dims):
        return vmem(), jax.ShapeDtypeStruct(dims, F32)

    def exchange(a, per_block):
        return lax.all_to_all(a, "ctx", 0, 0).reshape(BLOCKS * per_block, LANES)

    (sent,) = run(
        pack_kernel,
        "pack",
        [hbm(), hbm()],
        [stored(BLOCKS * (CHUNK + 1), LANES)],
        [
            scratch(steps_local, width),
            pltpu.VMEM((micro_rows, steps_local), jnp.int32),
            scratch(BLOCKS * (CHUNK + 1), LANES),
            pltpu.SemaphoreType.DMA((9,)),
        ],
        (
            pltpu.with_memory_space_constraint(features, pltpu.HBM),
            pltpu.with_memory_space_constraint(done_flags, pltpu.HBM),
        ),
    )
    received = lax.all_to_all(sent.reshape(BLOCKS, CHUNK + 1, 1, LANES), "ctx", 0, 0)
    received = received.reshape(BLOCKS * (CHUNK + 1), LANES)
    own, gain = run(
        rates_kernel,
        "rates",
        [vmem()] * 3,
        [out(2 * K, width), out(2 * K, width)],
        [],
        (-jnp.expm1(-decay_rate[0]), input_gain[0], output_gain[0]),
    )
    other = lax.ppermute(own, "sect", swap)
    head = value_head.reshape(1, width)
    aux, par, scale, power = run(
        tables_kernel,
        "tables",
        [smem()] * 2 + [vmem()] * 5,
        [
            out(AUX_ROWS, LANES),
            out(2, 2 * LANES, LANES),
            out(2 * K, LANES),
            out(2 * HALF, LANES),
        ],
        [],
        (traj_len, done_flags, own, other, gain, head, rewards),
    )
    sent_values, lift0, lift1, slope0, slope1, end0, flags, falls, rise = run(
        forward_kernel,
        "forward",
        [vmem()] * 2,
        [held(BLOCKS * PAYLOAD, LANES)]
        + [held(rows, LANES)] * 4
        + [held(K * 32, LANES)]
        + [held(BLOCKS, LANES)] * 2
        + [held(rows, LANES)],
        [scratch(rows, LANES)] * 3 + [scratch(K * 32, LANES)] * 4,
        (received, aux),
    )
    values = exchange(sent_values.reshape(BLOCKS, PAYLOAD, LANES), PAYLOAD)
    sent_carries, small = run(
        backward_kernel,
        "backward",
        [vmem()] * 10,
        [stored(BLOCKS, K, LANES), held(3 * K, LANES)],
        [scratch(rows, LANES)] * 2
        + [scratch(K * 32, LANES)] * 4
        + [scratch(BLOCKS, K, LANES), scratch(BLOCKS, LANES), pltpu.SemaphoreType.DMA((4,))],
        (values, aux, flags, falls, lift0, lift1, slope0, slope1, end0, rise),
    )
    carries = exchange(sent_carries, K)
    others = [lax.ppermute(small, "dp", [(i, i ^ far) for i in range(4)]) for far in (1, 2, 3)]
    by_tile = (
        features.reshape(micro_rows, steps_local // 8, 8, tiles, LANES)
        .transpose(0, 1, 3, 2, 4)
        .reshape(micro_rows, rows, LANES)
    )
    top, local_gs1, local_slope0 = run(
        local_forward_kernel,
        "local_forward",
        [vmem()] * 6,
        [out(rows, LANES)] * 3,
        [scratch(rows, LANES)] * 2 + [scratch(HALF, LANES)],
        (small, by_tile, values, par, power, value_head.reshape(tiles, LANES)),
    )
    local = (carries, par, top, local_gs1, local_slope0, power)
    half_rows = rows // 2
    keep0, send0, mine = run(
        first_half_kernel,
        "local_backward0",
        [vmem()] * 10,
        [out(half_rows, LANES), out(half_rows + 8, LANES), out(K, LANES)],
        [scratch(half_rows, LANES)] * 2,
        (*local, small, *others),
    )
    swapped0 = lax.ppermute(send0, "sect", swap)
    keep1, send1, placed0 = run(
        second_half_kernel,
        "local_backward1",
        [vmem()] * 7,
        [out(half_rows, LANES), out(half_rows, LANES), stored(2, 8, LANES, LANES)],
        [scratch(half_rows, LANES)] * 2 + [pltpu.SemaphoreType.DMA((8,))],
        (*local, keep0),
    )
    swapped1 = lax.ppermute(send1, "sect", swap)
    placed, grad_beta, grad_eta = run(
        place_kernel,
        "place",
        [vmem()] * 4 + [hbm()],
        [stored(2, 8, LANES, LANES), stored(K, HALF), stored(K, HALF)],
        [scratch(K, HALF)] * 2 + [pltpu.SemaphoreType.DMA((18,))],
        (keep1, swapped0, mine, scale, placed0),
        {4: 0},
    )
    (grads,) = run(
        finish_kernel,
        "finish",
        [vmem(), hbm()],
        [stored(2, 8, LANES, LANES)],
        [pltpu.SemaphoreType.DMA((8,))],
        (swapped1.reshape(8, HALF, LANES), placed),
        {1: 0},
    )
    grad_inputs = (
        grads.reshape(micro_rows, steps_local // 8, tiles, 8, LANES)
        .transpose(0, 1, 3, 2, 4)
        .reshape(1, micro_rows, steps_local, width)
    )
    return (grad_inputs, grad_beta[None], grad_eta[None])


def solution(mesh):
    placed = (
        P("dp", "ctx", None),
        P("dp", "ctx"),
        P("dp", "ctx"),
        P(),
        P("sect", None, None),
        P("sect", None, None),
        P("sect", None, None),
        P(),
    )
    return jax.shard_map(
        per_device,
        mesh=mesh,
        in_specs=placed,
        out_specs=(P("sect", "dp", "ctx", None), P("sect", None, "ctx"), P("sect", None, "ctx")),
        check_vma=False,
    )
```
